512 devices in a mesh: tile: 128 (over z, y, core), grp: 4 (over x).
Axes of the slice: x: 4, y: 8, z: 8, core: 2. Of those that a mesh axis runs over, the one named last changes fastest.
Arguments:
- kelvin_profile: float32 [90, 128, 256], P(None, 'tile'), may hold values from 0.5 to 1.5
- moisture_profile: float32 [90, 128, 256], P(None, 'tile'), may hold values from 0.1 to 3
- spreading_number: float32 [128, 256], P('tile'), may hold values from 0.05 to 0.24
- overhead_angle_measure: float32 [128, 256], P('tile'), may hold values from 0.2 to 1
- illuminated_mask: int32 [128, 256], P('tile'), may hold values 0 or 1
- radiating_tiles: int32 [32768, 1], P('tile'), may hold values from 0 to 127; in each aligned block of 256 rows (0 to 255, 256 to 511, ...) at most 4 rows name the same one
- cloudy_member_factors: float32 [224, 65536], P('grp', 'tile'), may hold values from 0.25 to 2
- arid_opacity_table: float32 [224, 90], P('grp'), may hold values from 0.003 to 0.2
- moisture_attenuation: float32 [224], P('grp'), may hold values from 0.003 to 0.05
- blackbody_share: float32 [224], P('grp'), may hold values from 0.3 to 3
- insolation_per_quadrature: float32 [224], P('grp'), may hold values from 0.3 to 3
Outputs:
- heating: float32 [90, 128, 256], P(None, 'tile')
- temp_next: float32 [90, 128, 256], P(None, 'tile')
- vapour_next: float32 [90, 128, 256], P(None, 'tile')
The draws below stay inside these ranges and needn't reach their ends.
Inputs may be any that keep to these rules, and one draw needn't show every extreme that they name: `radiating_tiles`: among the columns of one tile no owner is named more than 4 times, a bound that some block reaches.
All inputs are finite; a program needn't handle non-finite values. No bound on the sum of `illuminated_mask` on one device may be relied on, other than what follows from the above.
Results may differ from the reference program's by a relative error of at most 0.00025.
Values sent between devices are 32-bit elements; how exact they have to be, the bound alone decides.
A program may use at most 64 MiB of HBM per device.

```python
import math
import jax
import jax.numpy as jnp
import numpy as np
from jax import lax

STRATA_TOTAL = 90
NG = 224
BAND_SPAN = 256
ROWS_DEV = 1
PARALLEL_BANDS = 128
CAP = 4
N_TILE = 128


def touch_ends(values, stream_key, low, top_value):
    longest = values.shape.index(max(values.shape))
    spots = []
    for shift in (0, 1):
        where = [jax.random.randint(jax.random.fold_in(stream_key, axis), (), 0, length) for axis, length in enumerate(values.shape)]
        where[longest] = (where[longest] + shift) % values.shape[longest]
        spots.append(tuple(where))
    return values.at[spots[0]].set(low).at[spots[1]].set(top_value)


def levels(key, shape, cuts, least, high):
    def one(axis_at, shards_of):
        draws = jax.random.uniform(jax.random.fold_in(jax.random.fold_in(key, 6), axis_at), (shards_of,), jnp.float32, least / len(cuts), high / len(cuts))
        return jnp.repeat(jnp.exp(draws), shape[axis_at] // shards_of).reshape((-1,) + (1,) * (len(shape) - axis_at - 1))

    gain = one(*cuts[0])
    for cut in cuts[1:]:
        gain = gain * one(*cut)
    return gain


def shared_out(stream_key, own, number, rows, count, top, limit, slope):
    ranking = jax.random.permutation(stream_key, count)
    packed, common = portions_of(count, rows * top, limit, slope, True), portions_of(count, rows * top, limit, slope, False)
    places = jnp.arange(count)

    def named(lengths, offset_by):
        used = int((lengths > 0).sum())
        fixed = max(1, used // 4)
        shifted = fixed + (places - fixed + offset_by * (used - fixed)) % max(1, count - fixed)
        return jnp.zeros((count,), jnp.int32).at[ranking[jnp.where(places < fixed, places, shifted)]].set(jnp.asarray(lengths, jnp.int32))

    lengths = jnp.where(number % 4 == 0, named(packed, number // 4), named(common, number - number // 4 - 1))
    mixed = jax.random.permutation(jax.random.fold_in(own, 3), count)
    giver, taker = mixed[0:count // 2 * 2:2], mixed[1:count // 2 * 2:2]
    margin = jnp.minimum(lengths[giver] - 1, limit - lengths[taker]) // 2
    margin = jnp.where((giver == ranking[0]) | (taker == ranking[0]) | (lengths[taker] == 0), 0, jnp.maximum(margin, 0))
    shifted = jax.random.randint(jax.random.fold_in(own, 4), (count // 2,), 0, 1 << 20) % (margin + 1)
    lengths = lengths.at[giver].add(-shifted).at[taker].add(shifted)
    items = jnp.searchsorted(jnp.cumsum(lengths), jnp.arange(rows * top), side="right").astype(jnp.int32)
    listing = items.reshape(top, rows).T
    listing = listing[jax.random.permutation(jax.random.fold_in(own, 1), rows)]
    offset_by = jax.random.randint(jax.random.fold_in(own, 2), (rows, 1), 0, top)
    return jnp.take_along_axis(listing, (jnp.arange(top)[None, :] + offset_by) % top, axis=1)


def portions_of(number_of, total, limit, skew, full):
    portions = [(1 << 20) // math.isqrt(grade ** skew) + 1 for grade in range(1, number_of + 1)]
    largest = limit if full else min(limit, max(-(-total // number_of), total * portions[0] // sum(portions)))
    least = 1 if total - largest >= number_of - 1 else 0
    counts, surplus = [largest] + [least] * (number_of - 1), total - largest - least * (number_of - 1)
    while surplus > 0:
        movable = [i for i in range(1, number_of) if counts[i] < largest] or [i for i in range(1, number_of) if counts[i] < limit]
        pool, budget = sum([portions[i] for i in movable]), surplus
        for i in movable:
            more = min(limit - counts[i], max(1, budget * portions[i] // pool), surplus)
            counts[i] = counts[i] + more
            surplus = surplus - more
    return np.array(counts)


def setup_inputs(seed: int = 0) -> dict:
    seeds = jax.random.split(jax.random.key(seed), 12)
    kelvin_profile = jnp.clip(0.5 + 1.0 * jax.random.uniform(seeds[0], (STRATA_TOTAL, PARALLEL_BANDS, BAND_SPAN), jnp.float32) ** levels(seeds[0], (STRATA_TOTAL, PARALLEL_BANDS, BAND_SPAN), ((1, 128),), -0.2, 0.2), 0.5, 1.5)
    moisture_profile = jnp.clip(0.1 + 2.9 * jax.random.uniform(seeds[1], (STRATA_TOTAL, PARALLEL_BANDS, BAND_SPAN), jnp.float32) ** levels(seeds[1], (STRATA_TOTAL, PARALLEL_BANDS, BAND_SPAN), ((1, 128),), -0.2, 0.2), 0.1, 3.0)
    spreading_number = jnp.clip(0.05 + 0.19 * jax.random.uniform(seeds[2], (PARALLEL_BANDS, BAND_SPAN), jnp.float32) ** levels(seeds[2], (PARALLEL_BANDS, BAND_SPAN), ((0, 128),), -0.2, 0.2), 0.05, 0.24)
    overhead_angle_measure = jnp.clip(0.2 + 0.8 * jax.random.uniform(seeds[3], (PARALLEL_BANDS, BAND_SPAN), jnp.float32) ** levels(seeds[3], (PARALLEL_BANDS, BAND_SPAN), ((0, 128),), -0.2, 0.2), 0.2, 1.0)
    illuminated_mask = touch_ends((jax.random.randint(seeds[4], (PARALLEL_BANDS, BAND_SPAN), 0, 2) < 1).astype(jnp.int32), jax.random.fold_in(seeds[4], 1), 0, 1)
    radiating_tiles_keys = jax.random.split(jax.random.fold_in(seeds[5], 1), (PARALLEL_BANDS * BAND_SPAN) // (ROWS_DEV * BAND_SPAN))
    radiating_tiles_turns = jax.random.permutation(jax.random.fold_in(seeds[5], 3), (PARALLEL_BANDS * BAND_SPAN) // (ROWS_DEV * BAND_SPAN))
    radiating_tiles = jax.vmap(lambda own, number: shared_out(jax.random.fold_in(seeds[5], 2), own, number, ROWS_DEV * BAND_SPAN, N_TILE, 1, CAP, 1))(radiating_tiles_keys, radiating_tiles_turns).reshape((PARALLEL_BANDS * BAND_SPAN, 1))
    cloudy_member_factors = jnp.clip(0.25 + 1.75 * jax.random.uniform(seeds[6], (NG, N_TILE * N_TILE * CAP), jnp.float32) ** levels(seeds[6], (NG, N_TILE * N_TILE * CAP), ((0, 4), (1, 128)), -0.2, 0.2), 0.25, 2.0)
    arid_opacity_table = jnp.clip(jnp.exp(math.log(0.2) - 4.199705 * jax.random.uniform(seeds[7], (NG, STRATA_TOTAL), jnp.float32) ** levels(seeds[7], (NG, STRATA_TOTAL), ((0, 4),), -0.2, 0.2)), 0.003, 0.2)
    moisture_attenuation = jnp.clip(jnp.exp(math.log(0.05) - 2.8134107 * jax.random.uniform(seeds[8], (NG,), jnp.float32) ** levels(seeds[8], (NG,), ((0, 4),), -0.2, 0.2)), 0.003, 0.05)
    blackbody_share = jnp.clip(jnp.exp(math.log(3.0) - 2.3025851 * jax.random.uniform(seeds[9], (NG,), jnp.float32) ** levels(seeds[9], (NG,), ((0, 4),), -0.2, 0.2)), 0.3, 3.0)
    insolation_per_quadrature = jnp.clip(jnp.exp(math.log(3.0) - 2.3025851 * jax.random.uniform(seeds[10], (NG,), jnp.float32) ** levels(seeds[10], (NG,), ((0, 4),), -0.2, 0.2)), 0.3, 3.0)
    return dict(kelvin_profile=kelvin_profile, moisture_profile=moisture_profile, spreading_number=spreading_number, overhead_angle_measure=overhead_angle_measure, illuminated_mask=illuminated_mask, radiating_tiles=radiating_tiles, cloudy_member_factors=cloudy_member_factors, arid_opacity_table=arid_opacity_table, moisture_attenuation=moisture_attenuation, blackbody_share=blackbody_share, insolation_per_quadrature=insolation_per_quadrature)


def diffuse(atmosphere_variables, spreading_number):
    padded = jnp.pad(atmosphere_variables, ((0, 0), (0, 0), (1, 1), (0, 0)))
    eastern = jnp.roll(atmosphere_variables, -1, axis=3)
    western = jnp.roll(atmosphere_variables, 1, axis=3)
    return atmosphere_variables + spreading_number * (padded[:, :, :-2] + padded[:, :, 2:] + eastern + western - 4.0 * atmosphere_variables)


def evaluate_warming(kelvin_profile, moisture_profile, overhead_angle_value, illuminated_marker, profile_window, arid_multiplier, moisture_multiplier, radiance_share_table, sunshine_multiplier):
    gpoints, strata_mesh = arid_multiplier.shape
    bundle = math.gcd(gpoints, 4)
    bundles = gpoints // bundle
    lower_mask = (jnp.arange(strata_mesh)[None, :] < jnp.arange(strata_mesh + 1)[:, None]).astype(jnp.float32)
    upper_mask = 1.0 - lower_mask

    def layer_pass(pieces):
        dry_part, vapour_part, radiance_share_piece, solar_part, sub_part = pieces
        thickness = dry_part[:, :, None] + (vapour_part[:, None] * sub_part)[:, None, :] * moisture_profile[None]
        column_depth = jnp.einsum("lk,gkm->glm", lower_mask, thickness, precision=lax.Precision.HIGHEST)
        growth = jnp.exp(column_depth)
        damped = jnp.exp(-column_depth)
        infrared_radiance = radiance_share_piece[:, None, None] * kelvin_profile[None]
        downward = damped * jnp.einsum("lk,gkm->glm", lower_mask, infrared_radiance * growth[:, :strata_mesh] * jnp.expm1(thickness), precision=lax.Precision.HIGHEST)
        floor_term = infrared_radiance[:, strata_mesh - 1] * damped[:, strata_mesh]
        upward = growth * (floor_term[:, None, :] - jnp.einsum("lk,gkm->glm", upper_mask, infrared_radiance * damped[:, :strata_mesh] * jnp.expm1(-thickness), precision=lax.Precision.HIGHEST))
        sunbeam = solar_part[:, None, None] * illuminated_marker[None, None, :] * jnp.exp(-column_depth / overhead_angle_value[None, None, :])
        fluxes = downward - upward + sunbeam
        return jnp.sum(fluxes[:, :strata_mesh] - fluxes[:, 1:], axis=0)

    spectral = lax.map(layer_pass, (arid_multiplier.reshape(bundles, bundle, strata_mesh), moisture_multiplier.reshape(bundles, bundle), radiance_share_table.reshape(bundles, bundle), sunshine_multiplier.reshape(bundles, bundle), profile_window.reshape(bundles, bundle, profile_window.shape[1])))
    return jnp.sum(spectral, axis=0)


def reference(kelvin_profile, moisture_profile, spreading_number, overhead_angle_measure, illuminated_mask, radiating_tiles, cloudy_member_factors, arid_opacity_table, moisture_attenuation, blackbody_share, insolation_per_quadrature):
    atmosphere_variables = jnp.stack([kelvin_profile, moisture_profile])
    for repeat in range(2):
        atmosphere_variables = diffuse(atmosphere_variables, spreading_number)
    temp_dyn = atmosphere_variables[0]
    vapour_next = atmosphere_variables[1]
    columns = PARALLEL_BANDS * BAND_SPAN
    per_tile = ROWS_DEV * BAND_SPAN
    owner_ids = radiating_tiles[:, 0].reshape(N_TILE, per_tile)
    matches = (owner_ids[:, :, None] == jnp.arange(N_TILE, dtype=jnp.int32)[None, None, :]).astype(jnp.int32)
    position = jnp.sum((jnp.cumsum(matches, axis=1) - 1) * matches, axis=2)
    slot_index = (owner_ids * (N_TILE * CAP) + jnp.arange(N_TILE, dtype=jnp.int32)[:, None] * CAP + position).reshape(columns).astype(jnp.int32)
    picked = jnp.take(cloudy_member_factors, slot_index, axis=1)
    overhead_angle_value = overhead_angle_measure.reshape(columns)
    illuminated_marker = overhead_angle_value * illuminated_mask.reshape(columns).astype(jnp.float32)
    summed = evaluate_warming(temp_dyn.reshape(STRATA_TOTAL, columns), vapour_next.reshape(STRATA_TOTAL, columns), overhead_angle_value, illuminated_marker, picked, arid_opacity_table, moisture_attenuation, blackbody_share, insolation_per_quadrature)
    heating = (summed / NG).reshape(STRATA_TOTAL, PARALLEL_BANDS, BAND_SPAN)
    return heating, temp_dyn + heating, vapour_next
```

```python
import functools
import math

import jax
import jax.numpy as jnp
from jax import lax
from jax.experimental import pallas as pl
from jax.experimental.pallas import tpu as pltpu
from jax.sharding import PartitionSpec as P

F32 = jnp.float32
CORES, ROWS_Y = 2, 8
CAP = 4
SLOT = 64
MESH = pl.DeviceIdType.MESH
LOG2E = math.log2(math.e)


def remote(src, dst, send, recv, where):
    return pltpu.make_async_remote_copy(
        src_ref=src, dst_ref=dst, send_sem=send, recv_sem=recv, device_id=where, device_id_type=MESH
    )


def fold8(x):
    parts = [x[8 * k : 8 * k + 8] for k in range(x.shape[0] // 8)]
    while len(parts) > 1:
        parts = [sum(parts[k : k + 2][1:], parts[k]) for k in range(0, len(parts), 2)]
    return parts[0]


def radiation_kernel(
    dims,
    kel, moi, spread, mu, lit, owner, fac, arid, matt, share, insol,
    heat_o, temp_o, vap_o,
    facv, fact, out1, mid, out2, got,
    t0, q0, t1, q1, t2, q2, halo1, halo2, dts,
    dry, tbuf, mbuf, acc, flux, gbuf, wbuf,
    load_sem, h1s, h1r, h2s, h2r, p1s, p1r, p2s, p2r, gs, gr,
):
    tiles, ydim, groups = dims
    zcdim = tiles // ydim
    levels = t0.shape[0]
    gpts = arid.shape[0]
    cols = t0.shape[1]
    me, grp = lax.axis_index("tile"), lax.axis_index("grp")
    core, y, z = lax.rem(me, CORES), lax.rem(me // CORES, ydim), me // (CORES * ydim)
    zc = z * CORES + core

    def at_zc(k):
        other = lax.rem(zc + k, zcdim)
        return (other // CORES) * (CORES * ydim) + y * CORES + lax.rem(other, CORES), other

    def at_y(k):
        other = lax.rem(y + k, ydim)
        return z * (CORES * ydim) + other * CORES + core, other

    south, north = lax.rem(me + 1, tiles), lax.rem(me + tiles - 1, tiles)

    peers = [{"tile": at_zc(k)[0]} for k in range(1, zcdim)]
    peers += [{"tile": at_y(k)[0]} for k in range(1, ydim)]
    peers += [{"grp": lax.rem(grp + k, groups)} for k in range(1, groups)]
    peers += [{"tile": south}, {"tile": north}]
    barrier = pltpu.get_barrier_semaphore()
    for peer in peers:
        pl.semaphore_signal(barrier, inc=1, device_id=peer, device_id_type=MESH)

    loads = [
        pltpu.make_async_copy(src, dst, load_sem.at[k])
        for k, (src, dst) in enumerate(((fac, facv), (kel.at[:, 0, :], t0), (moi.at[:, 0, :], q0)))
    ]
    for load in loads:
        load.start()

    loads[0].wait()
    tall = jnp.concatenate([facv[...], jnp.zeros((128 - gpts, facv.shape[1]), F32)], axis=0)
    fact[...] = tall.T
    step = CORES * CAP
    for other in range(zcdim):
        base = (other // CORES) * (ydim * step) + (other % CORES) * CAP
        rows = [fact[pl.ds(base + r, ydim, stride=step), :] for r in range(CAP)]
        for half in range(CAP // 2):
            out1[other, :, 128 * half : 128 * half + 128] = rows[2 * half] + pltpu.roll(
                rows[2 * half + 1], SLOT, 1
            )

    pl.semaphore_wait(barrier, len(peers))

    def halo(sources, buffers, send, recv):
        copies = []
        for field, source in enumerate(sources):
            for side, where in enumerate((south, north)):
                k = 2 * field + side
                copies.append(
                    remote(source, buffers.at[side, field], send.at[k], recv.at[k], {"tile": where})
                )
        for copy in copies:
            copy.start()
        return copies

    first = halo((kel.at[:, 0, :], moi.at[:, 0, :]), halo1, h1s, h1r)

    phase1 = []
    for k in range(1, zcdim):
        where, other = at_zc(k)
        phase1.append(
            remote(out1.at[other], mid.at[zc], p1s.at[k], p1r.at[k], {"tile": where})
        )
        phase1[-1].start()
    mid[zc] = out1[zc]

    own = owner[...]
    place = (lax.rem(own // CORES, ydim) * zcdim + (own // (CORES * ydim)) * CORES + lax.rem(own, CORES))
    hot = jnp.where(lax.broadcasted_iota(jnp.int32, (tiles, cols), 0) == place, 1.0, 0.0)
    before = jnp.where(
        lax.broadcasted_iota(jnp.int32, (cols, cols), 0) < lax.broadcasted_iota(jnp.int32, (cols, cols), 1),
        1.0,
        0.0,
    )
    earlier = jnp.dot(hot.astype(jnp.bfloat16), before.astype(jnp.bfloat16), preferred_element_type=F32)
    rank = jnp.sum(hot * earlier, axis=0, keepdims=True)

    for l in range(levels):
        dry[l] = jnp.broadcast_to(arid[:, l : l + 1] * (-LOG2E), (gpts, 128))

    def column(row):
        return jnp.broadcast_to(row[...], (128, gpts)).T

    share_c, insol_c, matt_c = column(share), column(insol), column(matt) * (-LOG2E)
    inv_mu = 1.0 / mu[...]
    sun = mu[...] * lit[...].astype(F32)

    coefficient = spread[...]

    def advance(x, far_north, far_south):
        n = jnp.where(me > 0, far_north, 0.0)
        s = jnp.where(me < tiles - 1, far_south, 0.0)
        east, west = pltpu.roll(x, cols - 1, 1), pltpu.roll(x, 1, 1)
        return x + coefficient * (n + s + east + west - 4.0 * x)

    loads[1].wait()
    loads[2].wait()
    for copy in first:
        copy.wait_recv()
    t1[...] = advance(t0[...], halo1[0, 0], halo1[1, 0])
    q1[...] = advance(q0[...], halo1[0, 1], halo1[1, 1])
    second = halo((t1, q1), halo2, h2s, h2r)

    for copy in phase1:
        copy.wait_recv()
    for other in range(ydim):
        for zz in range(zcdim):
            out2[other, zz : zz + 1, :] = mid[zz, other : other + 1, :]
    phase2 = []
    for k in range(1, ydim):
        where, other = at_y(k)
        phase2.append(remote(out2.at[other], got.at[y], p2s.at[k], p2r.at[k], {"tile": where}))
        phase2[-1].start()
    got[y] = out2[y]

    for copy in second:
        copy.wait_recv()
    t2[...] = advance(t1[...], halo2[0, 0], halo2[1, 0])
    vapour = advance(q1[...], halo2[0, 1], halo2[1, 1])
    temp_o[...] = t2[...]
    vap_o[...] = vapour
    q2[...] = vapour.reshape(levels, 1, cols)
    dts[0] = -t2[0:1, :]
    dts[1:levels] = (t2[0 : levels - 1, :] - t2[1:levels, :]).reshape(levels - 1, 1, cols)
    dts[levels] = t2[levels - 1 : levels, :]

    for copy in phase2:
        copy.wait_recv()
    table = got[...].reshape(tiles, CAP * SLOT)
    picked = lax.dot_general(
        table, hot, (((0,), (0,)), ((), ())), precision=lax.Precision.HIGHEST, preferred_element_type=F32
    )
    chosen = jnp.zeros((gpts, cols), F32)
    for r in range(CAP):
        chosen = jnp.where(rank == float(r), picked[r * SLOT : r * SLOT + gpts], chosen)
    for half in range(cols // 128):
        wbuf[half] = chosen[:, 128 * half : 128 * half + 128] * matt_c

    reduce = []
    for half in range(cols // 128):
        lanes = pl.ds(128 * half, 128)
        w = wbuf[half]
        inv = inv_mu[:, 128 * half : 128 * half + 128]
        s0 = insol_c * sun[:, 128 * half : 128 * half + 128]

        def down(l, carry, w=w, inv=inv, lanes=lanes):
            d, s = carry
            a = dry[l] + w * q2[l, :, lanes]
            t, u = jnp.exp2(a), jnp.exp2(a * inv)
            m = t * d
            tbuf[l] = t
            mbuf[l] = m
            s = s * u
            acc[l + 1] = fold8(s)
            return m + dts[l + 1, :, lanes], s

        def up(i, e, lanes=lanes):
            l = levels - 1 - i
            acc[l + 1] += fold8((mbuf[l] - e) * share_c)
            return tbuf[l] * e + dts_minus(l, lanes)

        def dts_minus(l, lanes):
            return -dts[l, :, lanes]

        start = jnp.broadcast_to(dts[0, :, lanes], (gpts, 128))
        lax.fori_loop(0, levels, down, (start, s0), unroll=2)
        e = lax.fori_loop(0, levels, up, jnp.zeros((gpts, 128), F32), unroll=2)
        acc[0] = fold8(s0 - share_c * e)
        total = acc[:, 0, :]
        for k in range(1, 8):
            total = total + acc[:, k, :]
        flux[...] = total
        gbuf[half, grp] = flux[0:levels, :] - flux[1 : levels + 1, :]
        for k in range(1, groups):
            reduce.append(
                remote(
                    gbuf.at[half, grp], gbuf.at[half, grp], gs.at[half, k], gr.at[half, k],
                    {"grp": lax.rem(grp + k, groups)},
                )
            )
            reduce[-1].start()

    for half in range(cols // 128):
        for copy in reduce[half * (groups - 1) : (half + 1) * (groups - 1)]:
            copy.wait_recv()
        total = gbuf[half, 0]
        for k in range(1, groups):
            total = total + gbuf[half, k]
        heat_o[:, 128 * half : 128 * half + 128] = total * (1.0 / (groups * gpts))
    for copy in first + second + phase1 + phase2 + reduce:
        copy.wait_send()


def on_device(
    tiles, ydim, groups,
    kelvin, moisture, spread, mu, lit, owner, fac, arid, matt, share, insol,
):
    levels, _, cols = kelvin.shape
    gpts, slots = fac.shape
    zcdim = tiles // ydim
    vmem, hbm = pl.BlockSpec(memory_space=pltpu.VMEM), pl.BlockSpec(memory_space=pl.ANY)
    dma = pltpu.SemaphoreType.DMA
    field = pltpu.VMEM((levels, cols), F32)
    out = jax.ShapeDtypeStruct((levels, cols), F32)
    heat, temp, vap = pl.pallas_call(
        functools.partial(radiation_kernel, (tiles, ydim, groups)),
        out_shape=(out, out, out),
        in_specs=[hbm, hbm, vmem, vmem, vmem, vmem, hbm, vmem, vmem, vmem, vmem],
        out_specs=(vmem, vmem, vmem),
        scratch_shapes=[
            pltpu.VMEM((gpts, slots), F32),
            pltpu.VMEM((slots, 128), F32),
            pltpu.VMEM((zcdim, ydim, CAP * SLOT), F32),
            pltpu.VMEM((zcdim, ydim, CAP * SLOT), F32),
            pltpu.VMEM((ydim, zcdim, CAP * SLOT), F32),
            pltpu.VMEM((ydim, zcdim, CAP * SLOT), F32),
            field, field, field, field, field,
            pltpu.VMEM((levels, 1, cols), F32),
            pltpu.VMEM((2, 2, levels, cols), F32),
            pltpu.VMEM((2, 2, levels, cols), F32),
            pltpu.VMEM((levels + 1, 1, cols), F32),
            pltpu.VMEM((levels, gpts, 128), F32),
            pltpu.VMEM((levels, gpts, 128), F32),
            pltpu.VMEM((levels, gpts, 128), F32),
            pltpu.VMEM((levels + 1, 8, 128), F32),
            pltpu.VMEM((levels + 1, 128), F32),
            pltpu.VMEM((cols // 128, groups, levels, 128), F32),
            pltpu.VMEM((cols // 128, gpts, 128), F32),
            dma((3,)), dma((4,)), dma((4,)), dma((4,)), dma((4,)),
            dma((zcdim,)), dma((zcdim,)), dma((ydim,)), dma((ydim,)),
            dma((2, groups)), dma((2, groups)),
        ],
        compiler_params=pltpu.CompilerParams(
            collective_id=0, has_side_effects=True, vmem_limit_bytes=40 * 2**20
        ),
    )(
        kelvin, moisture, spread, mu, lit, owner.reshape(1, cols), fac, arid,
        matt.reshape(1, gpts), share.reshape(1, gpts), insol.reshape(1, gpts),
    )
    heat, temp, vap = (x.reshape(kelvin.shape) for x in (heat, temp, vap))
    return heat, temp + heat, vap


def solution(mesh):
    tiles, groups = mesh.shape["tile"], mesh.shape["grp"]
    ydim = min(ROWS_Y, tiles // (2 * CORES))
    wide, row = P(None, "tile", None), P("tile", None)
    in_specs = (
        wide, wide, row, row, row, row, P("grp", "tile"), P("grp", None), P("grp"), P("grp"), P("grp"),
    )
    return jax.shard_map(
        functools.partial(on_device, tiles, ydim, groups),
        mesh=mesh,
        in_specs=in_specs,
        out_specs=(wide, wide, wide),
        check_vma=False,
    )
```

```python
import functools
import math

import jax
import jax.numpy as jnp
from jax import lax
from jax.experimental import pallas as pl
from jax.experimental.pallas import tpu as pltpu
from jax.sharding import PartitionSpec as P

F32 = jnp.float32
CORES, ROWS_Y = 2, 8
CAP = 4
SLOT = 64
MESH = pl.DeviceIdType.MESH
LOG2E = math.log2(math.e)


def remote(src, dst, send, recv, where):
    return pltpu.make_async_remote_copy(
        src_ref=src, dst_ref=dst, send_sem=send, recv_sem=recv, device_id=where, device_id_type=MESH
    )


def fold8(x):
    parts = [x[8 * k : 8 * k + 8] for k in range(x.shape[0] // 8)]
    while len(parts) > 1:
        parts = [sum(parts[k : k + 2][1:], parts[k]) for k in range(0, len(parts), 2)]
    return parts[0]


def radiation_kernel(
    dims,
    kel, moi, spread_h, mu_h, lit_h, owner_h, fac, arid_h, matt_h, share_h, insol_h,
    heat_o, temp_o, vap_o,
    facv, spread, mu, lit, owner, arid, matt, share, insol, fact, out1, mid, out2, got,
    t0, q0, t1, q1, t2, q2, halo1, halo2, dts,
    dry, tbuf, mbuf, acc, flux, gbuf, wbuf,
    load_sem, h1s, h1r, h2s, h2r, p1s, p1r, p2s, p2r, gs, gr,
):
    tiles, ydim, groups = dims
    zcdim = tiles // ydim
    levels = t0.shape[0]
    gpts = arid.shape[0]
    cols = t0.shape[1]
    me, grp = lax.axis_index("tile"), lax.axis_index("grp")
    core, y, z = lax.rem(me, CORES), lax.rem(me // CORES, ydim), me // (CORES * ydim)
    zc = z * CORES + core

    def at_zc(k):
        other = lax.rem(zc + k, zcdim)
        return (other // CORES) * (CORES * ydim) + y * CORES + lax.rem(other, CORES), other

    def at_y(k):
        other = lax.rem(y + k, ydim)
        return z * (CORES * ydim) + other * CORES + core, other

    south, north = lax.rem(me + 1, tiles), lax.rem(me + tiles - 1, tiles)

    peers = [{"tile": at_zc(k)[0]} for k in range(1, zcdim)]
    peers += [{"tile": at_y(k)[0]} for k in range(1, ydim)]
    peers += [{"grp": lax.rem(grp + k, groups)} for k in range(1, groups)]
    peers += [{"tile": south}, {"tile": north}]
    barrier = pltpu.get_barrier_semaphore()
    for peer in peers:
        pl.semaphore_signal(barrier, inc=1, device_id=peer, device_id_type=MESH)

    loads = [
        pltpu.make_async_copy(src, dst, load_sem.at[k])
        for k, (src, dst) in enumerate(
            (
                (fac, facv), (kel.at[:, 0, :], t0), (moi.at[:, 0, :], q0), (owner_h, owner), (arid_h, arid),
                (matt_h, matt), (share_h, share), (insol_h, insol), (mu_h, mu), (lit_h, lit), (spread_h, spread),
            )
        )
    ]
    for load in loads:
        load.start()

    loads[0].wait()
    tall = jnp.concatenate([facv[...], jnp.zeros((128 - gpts, facv.shape[1]), F32)], axis=0)
    fact[...] = tall.T
    step = CORES * CAP
    for other in range(zcdim):
        base = (other // CORES) * (ydim * step) + (other % CORES) * CAP
        rows = [fact[pl.ds(base + r, ydim, stride=step), :] for r in range(CAP)]
        for half in range(CAP // 2):
            out1[other, :, 128 * half : 128 * half + 128] = rows[2 * half] + pltpu.roll(
                rows[2 * half + 1], SLOT, 1
            )

    pl.semaphore_wait(barrier, len(peers))

    def halo(sources, buffers, send, recv):
        copies = []
        for field, source in enumerate(sources):
            for side, where in enumerate((south, north)):
                k = 2 * field + side
                copies.append(
                    remote(source, buffers.at[side, field], send.at[k], recv.at[k], {"tile": where})
                )
        for copy in copies:
            copy.start()
        return copies

    first = halo((kel.at[:, 0, :], moi.at[:, 0, :]), halo1, h1s, h1r)

    phase1 = []
    for k in range(1, zcdim):
        where, other = at_zc(k)
        phase1.append(
            remote(out1.at[other], mid.at[zc], p1s.at[k], p1r.at[k], {"tile": where})
        )
        phase1[-1].start()
    mid[zc] = out1[zc]

    for load in loads[3:]:
        load.wait()
    own = owner[...]
    place = (lax.rem(own // CORES, ydim) * zcdim + (own // (CORES * ydim)) * CORES + lax.rem(own, CORES))
    hot = jnp.where(lax.broadcasted_iota(jnp.int32, (tiles, cols), 0) == place, 1.0, 0.0)
    before = jnp.where(
        lax.broadcasted_iota(jnp.int32, (cols, cols), 0) < lax.broadcasted_iota(jnp.int32, (cols, cols), 1),
        1.0,
        0.0,
    )
    earlier = jnp.dot(hot.astype(jnp.bfloat16), before.astype(jnp.bfloat16), preferred_element_type=F32)
    rank = jnp.sum(hot * earlier, axis=0, keepdims=True)

    for l in range(levels):
        dry[l] = jnp.broadcast_to(arid[:, l : l + 1] * (-LOG2E), (gpts, 128))

    def column(row):
        return jnp.broadcast_to(row[...], (128, gpts)).T

    share_c, insol_c, matt_c = column(share), column(insol), column(matt) * (-LOG2E)
    inv_mu = 1.0 / mu[...]
    sun = mu[...] * lit[...].astype(F32)

    coefficient = spread[...]

    def advance(x, far_north, far_south):
        n = jnp.where(me > 0, far_north, 0.0)
        s = jnp.where(me < tiles - 1, far_south, 0.0)
        east, west = pltpu.roll(x, cols - 1, 1), pltpu.roll(x, 1, 1)
        return x + coefficient * (n + s + east + west - 4.0 * x)

    loads[1].wait()
    loads[2].wait()
    for copy in first:
        copy.wait_recv()
    t1[...] = advance(t0[...], halo1[0, 0], halo1[1, 0])
    q1[...] = advance(q0[...], halo1[0, 1], halo1[1, 1])
    second = halo((t1, q1), halo2, h2s, h2r)

    for copy in phase1:
        copy.wait_recv()
    for other in range(ydim):
        for zz in range(zcdim):
            out2[other, zz : zz + 1, :] = mid[zz, other : other + 1, :]
    phase2 = []
    for k in range(1, ydim):
        where, other = at_y(k)
        phase2.append(remote(out2.at[other], got.at[y], p2s.at[k], p2r.at[k], {"tile": where}))
        phase2[-1].start()
    got[y] = out2[y]

    for copy in second:
        copy.wait_recv()
    t2[...] = advance(t1[...], halo2[0, 0], halo2[1, 0])
    vapour = advance(q1[...], halo2[0, 1], halo2[1, 1])
    temp_o[...] = t2[...]
    vap_o[...] = vapour
    q2[...] = vapour.reshape(levels, 1, cols)
    dts[0] = -t2[0:1, :]
    dts[1:levels] = (t2[0 : levels - 1, :] - t2[1:levels, :]).reshape(levels - 1, 1, cols)
    dts[levels] = t2[levels - 1 : levels, :]

    for copy in phase2:
        copy.wait_recv()
    table = got[...].reshape(tiles, CAP * SLOT)
    picked = lax.dot_general(
        table, hot, (((0,), (0,)), ((), ())), precision=lax.Precision.HIGHEST, preferred_element_type=F32
    )
    chosen = jnp.zeros((gpts, cols), F32)
    for r in range(CAP):
        chosen = jnp.where(rank == float(r), picked[r * SLOT : r * SLOT + gpts], chosen)
    for half in range(cols // 128):
        wbuf[half] = chosen[:, 128 * half : 128 * half + 128] * matt_c

    reduce = []
    for half in range(cols // 128):
        lanes = pl.ds(128 * half, 128)
        w = wbuf[half]
        inv = inv_mu[:, 128 * half : 128 * half + 128]
        s0 = insol_c * sun[:, 128 * half : 128 * half + 128]

        def down(l, carry, w=w, inv=inv, lanes=lanes):
            d, s = carry
            a = dry[l] + w * q2[l, :, lanes]
            t, u = jnp.exp2(a), jnp.exp2(a * inv)
            m = t * d
            tbuf[l] = t
            mbuf[l] = m
            s = s * u
            acc[l + 1] = fold8(s)
            return m + dts[l + 1, :, lanes], s

        def up(i, e, lanes=lanes):
            l = levels - 1 - i
            acc[l + 1] += fold8((mbuf[l] - e) * share_c)
            return tbuf[l] * e + dts_minus(l, lanes)

        def dts_minus(l, lanes):
            return -dts[l, :, lanes]

        start = jnp.broadcast_to(dts[0, :, lanes], (gpts, 128))
        lax.fori_loop(0, levels, down, (start, s0), unroll=10)
        e = lax.fori_loop(0, levels, up, jnp.zeros((gpts, 128), F32), unroll=10)
        acc[0] = fold8(s0 - share_c * e)
        total = acc[:, 0, :]
        for k in range(1, 8):
            total = total + acc[:, k, :]
        flux[...] = total
        gbuf[half, grp] = flux[0:levels, :] - flux[1 : levels + 1, :]
        for k in range(1, groups):
            reduce.append(
                remote(
                    gbuf.at[half, grp], gbuf.at[half, grp], gs.at[half, k], gr.at[half, k],
                    {"grp": lax.rem(grp + k, groups)},
                )
            )
            reduce[-1].start()

    for half in range(cols // 128):
        for copy in reduce[half * (groups - 1) : (half + 1) * (groups - 1)]:
            copy.wait_recv()
        total = gbuf[half, 0]
        for k in range(1, groups):
            total = total + gbuf[half, k]
        heat_o[:, 128 * half : 128 * half + 128] = total * (1.0 / (groups * gpts))
    for copy in first + second + phase1 + phase2 + reduce:
        copy.wait_send()


def finish_kernel(heat, temp, vap, heat_o, temp_o, vap_o, heat_v, temp_v, vap_v, sem):
    copies = []
    for k, (value, buffer, out) in enumerate(
        (
            (vap[...], vap_v, vap_o),
            (heat[...], heat_v, heat_o),
            (temp[...] + heat[...], temp_v, temp_o),
        )
    ):
        buffer[...] = value.reshape(buffer.shape)
        copies.append(pltpu.make_async_copy(buffer, out, sem.at[k]))
        copies[-1].start()
    for copy in copies:
        copy.wait()


def on_device(
    tiles, ydim, groups,
    kelvin, moisture, spread, mu, lit, owner, fac, arid, matt, share, insol,
):
    levels, _, cols = kelvin.shape
    gpts, slots = fac.shape
    zcdim = tiles // ydim
    vmem, hbm = pl.BlockSpec(memory_space=pltpu.VMEM), pl.BlockSpec(memory_space=pltpu.HBM)
    dma = pltpu.SemaphoreType.DMA
    field = pltpu.VMEM((levels, cols), F32)
    out = jax.ShapeDtypeStruct((levels, cols), F32)
    heat, temp, vap = pl.pallas_call(
        functools.partial(radiation_kernel, (tiles, ydim, groups)),
        out_shape=(out, out, out),
        in_specs=[hbm] * 11,
        out_specs=(vmem, vmem, vmem),
        scratch_shapes=[
            pltpu.VMEM((gpts, slots), F32),
            pltpu.VMEM((1, cols), F32), pltpu.VMEM((1, cols), F32), pltpu.VMEM((1, cols), jnp.int32), pltpu.VMEM((1, cols), jnp.int32),
            pltpu.VMEM((gpts, levels), F32), pltpu.VMEM((1, gpts), F32), pltpu.VMEM((1, gpts), F32), pltpu.VMEM((1, gpts), F32),
            pltpu.VMEM((slots, 128), F32),
            pltpu.VMEM((zcdim, ydim, CAP * SLOT), F32),
            pltpu.VMEM((zcdim, ydim, CAP * SLOT), F32),
            pltpu.VMEM((ydim, zcdim, CAP * SLOT), F32),
            pltpu.VMEM((ydim, zcdim, CAP * SLOT), F32),
            field, field, field, field, field,
            pltpu.VMEM((levels, 1, cols), F32),
            pltpu.VMEM((2, 2, levels, cols), F32),
            pltpu.VMEM((2, 2, levels, cols), F32),
            pltpu.VMEM((levels + 1, 1, cols), F32),
            pltpu.VMEM((levels, gpts, 128), F32),
            pltpu.VMEM((levels, gpts, 128), F32),
            pltpu.VMEM((levels, gpts, 128), F32),
            pltpu.VMEM((levels + 1, 8, 128), F32),
            pltpu.VMEM((levels + 1, 128), F32),
            pltpu.VMEM((cols // 128, groups, levels, 128), F32),
            pltpu.VMEM((cols // 128, gpts, 128), F32),
            dma((11,)), dma((4,)), dma((4,)), dma((4,)), dma((4,)),
            dma((zcdim,)), dma((zcdim,)), dma((ydim,)), dma((ydim,)),
            dma((2, groups)), dma((2, groups)),
        ],
        compiler_params=pltpu.CompilerParams(
            collective_id=0, has_side_effects=True, vmem_limit_bytes=56 * 2**20
        ),
    )(
        kelvin, moisture, spread, mu, lit, owner.reshape(1, cols), fac, arid,
        matt.reshape(1, gpts), share.reshape(1, gpts), insol.reshape(1, gpts),
    )
    out = jax.ShapeDtypeStruct(kelvin.shape, F32)
    return pl.pallas_call(
        finish_kernel,
        out_shape=(out, out, out),
        in_specs=[vmem] * 3,
        out_specs=(hbm,) * 3,
        scratch_shapes=[pltpu.VMEM(kelvin.shape, F32)] * 3 + [dma((3,))],
    )(heat, temp, vap)


def solution(mesh):
    tiles, groups = mesh.shape["tile"], mesh.shape["grp"]
    ydim = min(ROWS_Y, tiles // (2 * CORES))
    wide, row = P(None, "tile", None), P("tile", None)
    in_specs = (
        wide, wide, row, row, row, row, P("grp", "tile"), P("grp", None), P("grp"), P("grp"), P("grp"),
    )
    return jax.shard_map(
        functools.partial(on_device, tiles, ydim, groups),
        mesh=mesh,
        in_specs=in_specs,
        out_specs=(wide, wide, wide),
        check_vma=False,
    )
```

```python
import functools
import math

import jax
import jax.numpy as jnp
from jax import lax
from jax.experimental import pallas as pl
from jax.experimental.pallas import tpu as pltpu
from jax.sharding import PartitionSpec as P

F32 = jnp.float32
CORES, ROWS_Y = 2, 8
CAP = 4
SLOT = 64
MESH = pl.DeviceIdType.MESH
LOG2E = math.log2(math.e)


def remote(src, dst, send, recv, where):
    return pltpu.make_async_remote_copy(
        src_ref=src, dst_ref=dst, send_sem=send, recv_sem=recv, device_id=where, device_id_type=MESH
    )


def far_first(n):
    return sorted(range(n), key=lambda d: -min(d, n - d))


def pair(rows, base, count, step):
    low, high = (rows[pl.ds(base + r, count, stride=step), :] for r in (0, 1))
    return low + pltpu.roll(high, SLOT, 1)


def fold8(x):
    parts = [x[8 * k : 8 * k + 8] for k in range(x.shape[0] // 8)]
    while len(parts) > 1:
        parts = [sum(parts[k : k + 2][1:], parts[k]) for k in range(0, len(parts), 2)]
    return parts[0]


def radiation_kernel(
    dims,
    kel, moi, spread_h, mu_h, lit_h, owner_h, fac, arid_h, matt_h, share_h, insol_h,
    heat_o, temp_o, vap_o,
    facv, spread, mu, lit, owner, arid, matt, share, insol, fact, out1a, out1b, mida, midb, out2a, out2b, gota, gotb, hots,
    t0, q0, t1, q1, t2, q2, halo1, halo2, dts,
    dry, tbuf, mbuf, acc, flux, gbuf, wbuf,
    load_sem, h1s, h1r, h2s, h2r, p1s, p1r, p2s, p2r, gs, gr,
):
    tiles, ydim, groups = dims
    zcdim, ycdim = tiles // ydim, CORES * ydim
    levels = t0.shape[0]
    gpts = arid.shape[0]
    cols = t0.shape[1]
    me, grp = lax.axis_index("tile"), lax.axis_index("grp")
    core, y, z = lax.rem(me, CORES), lax.rem(me // CORES, ydim), me // (CORES * ydim)
    zdim = zcdim // CORES
    zc, yc = z * CORES + core, y * CORES + core

    def tile_of(a, b, c):
        return (a * ydim + b) * CORES + c

    near = [(d, c) for d in far_first(zdim) for c in (1, 0) if d or c]
    at_zc = []
    for d, c in near:
        zz, cc = lax.rem(z + d, zdim), lax.rem(core + c, CORES)
        at_zc.append((tile_of(zz, y, cc), zz * CORES + cc))
    at_yc = []
    for d, c in [(d, c) for d in far_first(ydim) for c in (1, 0) if d or c]:
        yy, cc = lax.rem(y + d, ydim), lax.rem(core + c, CORES)
        at_yc.append((tile_of(z, yy, cc), yy * CORES + cc))
    at_y = [(tile_of(z, lax.rem(y + d, ydim), core), lax.rem(y + d, ydim)) for d in far_first(ydim) if d]
    at_z = [(tile_of(lax.rem(z + d, zdim), y, core), lax.rem(z + d, zdim)) for d in far_first(zdim) if d]
    across = [k for k in far_first(groups) if k]

    south, north = lax.rem(me + 1, tiles), lax.rem(me + tiles - 1, tiles)

    peers = [{"tile": south}, {"tile": north}]
    peers += [{"tile": where} for where, _ in at_zc] + [{"tile": where} for where, _ in at_yc]
    peers += [{"grp": lax.rem(grp + k, groups)} for k in across]
    barrier = pltpu.get_barrier_semaphore()
    for peer in peers:
        pl.semaphore_signal(barrier, inc=1, device_id=peer, device_id_type=MESH)

    loads = [
        pltpu.make_async_copy(src, dst, load_sem.at[k])
        for k, (src, dst) in enumerate(
            (
                (fac, facv), (kel.at[:, 0, :], t0), (moi.at[:, 0, :], q0), (owner_h, owner), (arid_h, arid),
                (matt_h, matt), (share_h, share), (insol_h, insol), (mu_h, mu), (lit_h, lit), (spread_h, spread),
            )
        )
    ]
    for load in loads:
        load.start()

    loads[0].wait()
    tall = jnp.concatenate([facv[...], jnp.zeros((128 - gpts, facv.shape[1]), F32)], axis=0)
    fact[...] = tall.T
    step = CORES * CAP
    for k in range(zcdim):
        base = (k // CORES) * (ydim * step) + (k % CORES) * CAP
        out1a[k] = pair(fact, base, ydim, step)
    for k in range(ycdim):
        out1b[k] = pair(fact, k * CAP + 2, zdim, ydim * step)

    pl.semaphore_wait(barrier, len(peers))

    def halo(field, source, buffers, send, recv):
        copies = []
        for side, where in enumerate((south, north)):
            k = 2 * field + side
            copies.append(
                remote(source, buffers.at[side, field], send.at[k], recv.at[k], {"tile": where})
            )
            copies[-1].start()
        return copies

    first = [
        halo(field, source.at[:, 0, :], halo1, h1s, h1r) for field, source in enumerate((moi, kel))
    ]

    def spread_out(source, target, mine, partners, send, recv):
        copies = []
        for k, (where, other) in enumerate(partners):
            copies.append(
                remote(source.at[other], target.at[mine], send.at[k], recv.at[k], {"tile": where})
            )
            copies[-1].start()
        return copies

    phase1 = spread_out(out1a, mida, zc, at_zc, p1s.at[0], p1r.at[0])
    phase1 += spread_out(out1b, midb, yc, at_yc, p1s.at[1], p1r.at[1])
    mida[zc] = out1a[zc]
    midb[yc] = out1b[yc]

    for load in loads[3:]:
        load.wait()
    own = owner[...]
    place = lax.rem(own // CORES, ydim) * zcdim + (own // ycdim) * CORES + lax.rem(own, CORES)
    listed = lax.broadcasted_iota(jnp.int32, (tiles, cols), 0)
    hot = jnp.where(listed == own, 1.0, 0.0)
    before = jnp.where(
        lax.broadcasted_iota(jnp.int32, (cols, cols), 0) < lax.broadcasted_iota(jnp.int32, (cols, cols), 1),
        1.0,
        0.0,
    )
    earlier = jnp.dot(hot.astype(jnp.bfloat16), before.astype(jnp.bfloat16), preferred_element_type=F32)
    rank = jnp.sum(hot * earlier, axis=0, keepdims=True)
    hots[0:tiles] = jnp.where((listed == place) & (rank < 1.5), 1.0, 0.0).astype(jnp.bfloat16)
    hots[tiles : 2 * tiles] = jnp.where((listed == own) & (rank > 1.5), 1.0, 0.0).astype(jnp.bfloat16)
    odd = (rank == 1.0) | (rank == 3.0)

    for l in range(levels):
        dry[l] = jnp.broadcast_to(arid[:, l : l + 1] * (-LOG2E), (gpts, 128))

    def column(row):
        return jnp.broadcast_to(row[...], (128, gpts)).T

    share_c, insol_c, matt_c = column(share), column(insol), column(matt) * (-LOG2E)
    inv_mu = 1.0 / mu[...]
    sun = mu[...] * lit[...].astype(F32)

    coefficient = spread[...]

    def advance(x, far_north, far_south):
        n = jnp.where(me > 0, far_north, 0.0)
        s = jnp.where(me < tiles - 1, far_south, 0.0)
        east, west = pltpu.roll(x, cols - 1, 1), pltpu.roll(x, 1, 1)
        return x + coefficient * (n + s + east + west - 4.0 * x)

    loads[1].wait()
    loads[2].wait()

    def arrive(copies):
        for copy in copies:
            copy.wait_recv()

    arrive(first[0])
    q1[...] = advance(q0[...], halo1[0, 0], halo1[1, 0])
    second = [halo(0, q1, halo2, h2s, h2r)]
    arrive(first[1])
    t1[...] = advance(t0[...], halo1[0, 1], halo1[1, 1])
    second.append(halo(1, t1, halo2, h2s, h2r))

    arrive(phase1)
    for k in range(ydim):
        out2a[k] = mida.reshape(tiles, 2 * SLOT)[pl.ds(k, zcdim, stride=ydim), :]
    for k in range(zdim):
        out2b[k] = midb.reshape(tiles, 2 * SLOT)[pl.ds(k, ycdim, stride=zdim), :]
    phase2 = spread_out(out2a, gota, y, at_y, p2s.at[0], p2r.at[0])
    phase2 += spread_out(out2b, gotb, z, at_z, p2s.at[1], p2r.at[1])
    gota[y] = out2a[y]
    gotb[z] = out2b[z]

    arrive(second[0])
    vapour = advance(q1[...], halo2[0, 0], halo2[1, 0]).reshape(levels, 1, cols)
    q2[...] = vapour
    vap_o[...] = vapour
    arrive(second[1])
    t2[...] = advance(t1[...], halo2[0, 1], halo2[1, 1])
    dts[0] = -t2[0:1, :]
    dts[1:levels] = (t2[0 : levels - 1, :] - t2[1:levels, :]).reshape(levels - 1, 1, cols)
    dts[levels] = t2[levels - 1 : levels, :]

    arrive(phase2)
    table = jnp.concatenate(
        [gota[...].reshape(tiles, 2 * SLOT), gotb[...].reshape(tiles, 2 * SLOT)], axis=0
    )
    picked = jnp.zeros((2 * SLOT, cols), F32)
    for _ in range(3):
        part = table.astype(jnp.bfloat16)
        table = table - part.astype(F32)
        picked = picked + lax.dot_general(
            part, hots[...], (((0,), (0,)), ((), ())), preferred_element_type=F32
        )
    chosen = jnp.where(odd, picked[SLOT : SLOT + gpts], picked[0:gpts])
    for half in range(cols // 128):
        wbuf[half] = chosen[:, 128 * half : 128 * half + 128] * matt_c

    reduce = []
    for half in range(cols // 128):
        lanes = pl.ds(128 * half, 128)
        w = wbuf[half]
        inv = inv_mu[:, 128 * half : 128 * half + 128]
        s0 = insol_c * sun[:, 128 * half : 128 * half + 128]

        def down(l, carry, w=w, inv=inv, lanes=lanes):
            d, s = carry
            a = dry[l] + w * q2[l, :, lanes]
            t, u = jnp.exp2(a), jnp.exp2(a * inv)
            m = t * d
            tbuf[l] = t
            mbuf[l] = m
            s = s * u
            acc[l + 1] = fold8(s)
            return m + dts[l + 1, :, lanes], s

        def up(i, e, lanes=lanes):
            l = levels - 1 - i
            acc[l + 1] += fold8((mbuf[l] - e) * share_c)
            return tbuf[l] * e + dts_minus(l, lanes)

        def dts_minus(l, lanes):
            return -dts[l, :, lanes]

        start = jnp.broadcast_to(dts[0, :, lanes], (gpts, 128))
        lax.fori_loop(0, levels, down, (start, s0), unroll=10)
        e = lax.fori_loop(0, levels, up, jnp.zeros((gpts, 128), F32), unroll=10)
        acc[0] = fold8(s0 - share_c * e)
        total = acc[:, 0, :]
        for k in range(1, 8):
            total = total + acc[:, k, :]
        flux[...] = total
        gbuf[half, grp] = flux[0:levels, :] - flux[1 : levels + 1, :]
        for k in across:
            reduce.append(
                remote(
                    gbuf.at[half, grp], gbuf.at[half, grp], gs.at[half, k], gr.at[half, k],
                    {"grp": lax.rem(grp + k, groups)},
                )
            )
            reduce[-1].start()

    for half in range(cols // 128):
        for copy in reduce[half * (groups - 1) : (half + 1) * (groups - 1)]:
            copy.wait_recv()
        total = gbuf[half, 0]
        for k in range(1, groups):
            total = total + gbuf[half, k]
        lanes = pl.ds(128 * half, 128)
        total = total * (1.0 / (groups * gpts))
        heat_o[:, :, lanes] = total.reshape(levels, 1, 128)
        temp_o[:, :, lanes] = (t2[:, lanes] + total).reshape(levels, 1, 128)
    for copy in first[0] + first[1] + second[0] + second[1] + phase1 + phase2 + reduce:
        copy.wait_send()


def finish_kernel(heat, temp, vap, heat_o, temp_o, vap_o, sem):
    copies = [
        pltpu.make_async_copy(value, out, sem.at[k])
        for k, (value, out) in enumerate(((heat, heat_o), (temp, temp_o), (vap, vap_o)))
    ]
    for copy in copies:
        copy.start()
    for copy in copies:
        copy.wait()


def on_device(
    tiles, ydim, groups,
    kelvin, moisture, spread, mu, lit, owner, fac, arid, matt, share, insol,
):
    levels, _, cols = kelvin.shape
    gpts, slots = fac.shape
    zcdim, ycdim = tiles // ydim, CORES * ydim
    zdim = zcdim // CORES
    most = max(zcdim, ycdim)
    vmem, hbm = pl.BlockSpec(memory_space=pltpu.VMEM), pl.BlockSpec(memory_space=pltpu.HBM)
    dma = pltpu.SemaphoreType.DMA
    field = pltpu.VMEM((levels, cols), F32)
    out = pltpu.VMEM((levels, 1, cols), F32)
    heat, temp, vap = pl.pallas_call(
        functools.partial(radiation_kernel, (tiles, ydim, groups)),
        out_shape=(out, out, out),
        in_specs=[hbm] * 11,
        out_specs=(vmem, vmem, vmem),
        scratch_shapes=[
            pltpu.VMEM((gpts, slots), F32),
            pltpu.VMEM((1, cols), F32), pltpu.VMEM((1, cols), F32), pltpu.VMEM((1, cols), jnp.int32), pltpu.VMEM((1, cols), jnp.int32),
            pltpu.VMEM((gpts, levels), F32), pltpu.VMEM((1, gpts), F32), pltpu.VMEM((1, gpts), F32), pltpu.VMEM((1, gpts), F32),
            pltpu.VMEM((slots, 128), F32),
            pltpu.VMEM((zcdim, ydim, 128), F32), pltpu.VMEM((ycdim, zdim, 128), F32),
            pltpu.VMEM((zcdim, ydim, 128), F32), pltpu.VMEM((ycdim, zdim, 128), F32),
            pltpu.VMEM((ydim, zcdim, 128), F32), pltpu.VMEM((zdim, ycdim, 128), F32),
            pltpu.VMEM((ydim, zcdim, 128), F32), pltpu.VMEM((zdim, ycdim, 128), F32),
            pltpu.VMEM((2 * tiles, cols), jnp.bfloat16),
            field, field, field, field, field,
            pltpu.VMEM((levels, 1, cols), F32),
            pltpu.VMEM((2, 2, levels, cols), F32),
            pltpu.VMEM((2, 2, levels, cols), F32),
            pltpu.VMEM((levels + 1, 1, cols), F32),
            pltpu.VMEM((levels, gpts, 128), F32),
            pltpu.VMEM((levels, gpts, 128), F32),
            pltpu.VMEM((levels, gpts, 128), F32),
            pltpu.VMEM((levels + 1, 8, 128), F32),
            pltpu.VMEM((levels + 1, 128), F32),
            pltpu.VMEM((cols // 128, groups, levels, 128), F32),
            pltpu.VMEM((cols // 128, gpts, 128), F32),
            dma((11,)), dma((4,)), dma((4,)), dma((4,)), dma((4,)),
            dma((2, most)), dma((2, most)), dma((2, most)), dma((2, most)),
            dma((2, groups)), dma((2, groups)),
        ],
        compiler_params=pltpu.CompilerParams(
            collective_id=0, has_side_effects=True, vmem_limit_bytes=56 * 2**20
        ),
    )(
        kelvin, moisture, spread, mu, lit, owner.reshape(1, cols), fac, arid,
        matt.reshape(1, gpts), share.reshape(1, gpts), insol.reshape(1, gpts),
    )
    out = jax.ShapeDtypeStruct(kelvin.shape, F32)
    return pl.pallas_call(
        finish_kernel,
        out_shape=(out, out, out),
        in_specs=[vmem] * 3,
        out_specs=(hbm,) * 3,
        scratch_shapes=[dma((3,))],
        compiler_params=pltpu.CompilerParams(vmem_limit_bytes=2**20),
    )(heat, temp, vap)


def solution(mesh):
    tiles, groups = mesh.shape["tile"], mesh.shape["grp"]
    ydim = min(ROWS_Y, tiles // (2 * CORES))
    wide, row = P(None, "tile", None), P("tile", None)
    in_specs = (
        wide, wide, row, row, row, row, P("grp", "tile"), P("grp", None), P("grp"), P("grp"), P("grp"),
    )
    return jax.shard_map(
        functools.partial(on_device, tiles, ydim, groups),
        mesh=mesh,
        in_specs=in_specs,
        out_specs=(wide, wide, wide),
        check_vma=False,
    )
```

```python
import functools
import math

import jax
import jax.numpy as jnp
from jax import lax
from jax.experimental import pallas as pl
from jax.experimental.pallas import tpu as pltpu
from jax.sharding import PartitionSpec as P

F32 = jnp.float32
CORES, ROWS_Y = 2, 8
CAP = 4
SLOT = 64
MESH = pl.DeviceIdType.MESH
LOG2E = math.log2(math.e)


def remote(src, dst, send, recv, where):
    return pltpu.make_async_remote_copy(
        src_ref=src, dst_ref=dst, send_sem=send, recv_sem=recv, device_id=where, device_id_type=MESH
    )


def far_first(n):
    return sorted(range(n), key=lambda d: -min(d, n - d))


def pair(rows, base, count, step):
    low, high = (rows[pl.ds(base + r, count, stride=step), :] for r in (0, 1))
    return low + pltpu.roll(high, SLOT, 1)


def fold8(x):
    parts = [x[8 * k : 8 * k + 8] for k in range(x.shape[0] // 8)]
    while len(parts) > 1:
        parts = [sum(parts[k : k + 2][1:], parts[k]) for k in range(0, len(parts), 2)]
    return parts[0]


def radiation_kernel(
    dims,
    kel, moi, spread_h, mu_h, lit_h, owner_h, fac, arid_h, matt_h, share_h, insol_h,
    heat_o, temp_o, vap_o,
    facv, spread, mu, lit, owner, arid, matt, share, insol, fact, out1a, out1b, mida, midb, out2a, out2b, gota, gotb, hots,
    mine, halo, coefs, q2, t2, dts,
    dry, tbuf, mbuf, acc, flux, gbuf, wbuf,
    load_sem, hs, hr, cs, cr, xs, xr, vap_sem, p1s, p1r, p2s, p2r, gs, gr,
):
    tiles, ydim, groups = dims
    zcdim, ycdim = tiles // ydim, CORES * ydim
    levels, _, cols = kel.shape
    part = halo.shape[2]
    gap = groups * part - levels
    gpts = arid.shape[0]
    me, grp = lax.axis_index("tile"), lax.axis_index("grp")
    core, y, z = lax.rem(me, CORES), lax.rem(me // CORES, ydim), me // (CORES * ydim)
    zdim = zcdim // CORES
    zc, yc = z * CORES + core, y * CORES + core

    def tile_of(a, b, c):
        return (a * ydim + b) * CORES + c

    near = [(d, c) for d in far_first(zdim) for c in (1, 0) if d or c]
    at_zc = []
    for d, c in near:
        zz, cc = lax.rem(z + d, zdim), lax.rem(core + c, CORES)
        at_zc.append((tile_of(zz, y, cc), zz * CORES + cc))
    at_yc = []
    for d, c in [(d, c) for d in far_first(ydim) for c in (1, 0) if d or c]:
        yy, cc = lax.rem(y + d, ydim), lax.rem(core + c, CORES)
        at_yc.append((tile_of(z, yy, cc), yy * CORES + cc))
    at_y = [(tile_of(z, lax.rem(y + d, ydim), core), lax.rem(y + d, ydim)) for d in far_first(ydim) if d]
    at_z = [(tile_of(lax.rem(z + d, zdim), y, core), lax.rem(z + d, zdim)) for d in far_first(zdim) if d]
    across = [k for k in far_first(groups) if k]

    rows = [(lax.rem(me + tiles - d, tiles), k) for k, d in enumerate((-2, -1, 1, 2))]
    level = jnp.minimum(grp * part, levels - part)

    peers = [{"tile": where} for where, _ in rows]
    peers += [{"tile": where} for where, _ in at_zc] + [{"tile": where} for where, _ in at_yc]
    peers += [{"grp": lax.rem(grp + k, groups)} for k in across]
    barrier = pltpu.get_barrier_semaphore()
    for peer in peers:
        pl.semaphore_signal(barrier, inc=1, device_id=peer, device_id_type=MESH)

    loads = [
        pltpu.make_async_copy(src, dst, load_sem.at[k])
        for k, (src, dst) in enumerate(
            (
                (fac, facv), (moi.at[pl.ds(level, part), 0, :], mine.at[0]), (kel.at[pl.ds(level, part), 0, :], mine.at[1]),
                (owner_h, owner), (arid_h, arid), (matt_h, matt), (share_h, share), (insol_h, insol), (mu_h, mu),
                (lit_h, lit), (spread_h, spread),
            )
        )
    ]
    for load in loads:
        load.start()

    loads[0].wait()
    tall = jnp.concatenate([facv[...], jnp.zeros((128 - gpts, facv.shape[1]), F32)], axis=0)
    fact[...] = tall.T
    step = CORES * CAP
    for k in range(zcdim):
        base = (k // CORES) * (ydim * step) + (k % CORES) * CAP
        out1a[k] = pair(fact, base, ydim, step)
    for k in range(ycdim):
        out1b[k] = pair(fact, k * CAP + 2, zdim, ydim * step)

    pl.semaphore_wait(barrier, len(peers))

    halos = []
    for where, k in rows:
        for field, source in enumerate((moi, kel)):
            halos.append(
                remote(
                    source.at[pl.ds(level, part), 0, :], halo.at[k, field], hs.at[k, field], hr.at[k, field],
                    {"tile": where},
                )
            )
        if k in (1, 2):
            halos.append(remote(spread_h, coefs.at[k - 1], cs.at[k - 1], cr.at[k - 1], {"tile": where}))
    for copy in halos:
        copy.start()

    def spread_out(source, target, mine, partners, send, recv):
        copies = []
        for k, (where, other) in enumerate(partners):
            copies.append(
                remote(source.at[other], target.at[mine], send.at[k], recv.at[k], {"tile": where})
            )
            copies[-1].start()
        return copies

    phase1 = spread_out(out1a, mida, zc, at_zc, p1s.at[0], p1r.at[0])
    phase1 += spread_out(out1b, midb, yc, at_yc, p1s.at[1], p1r.at[1])
    mida[zc] = out1a[zc]
    midb[yc] = out1b[yc]

    for load in loads[3:]:
        load.wait()
    own = owner[...]
    place = lax.rem(own // CORES, ydim) * zcdim + (own // ycdim) * CORES + lax.rem(own, CORES)
    listed = lax.broadcasted_iota(jnp.int32, (tiles, cols), 0)
    hot = jnp.where(listed == own, 1.0, 0.0)
    before = jnp.where(
        lax.broadcasted_iota(jnp.int32, (cols, cols), 0) < lax.broadcasted_iota(jnp.int32, (cols, cols), 1),
        1.0,
        0.0,
    )
    earlier = jnp.dot(hot.astype(jnp.bfloat16), before.astype(jnp.bfloat16), preferred_element_type=F32)
    rank = jnp.sum(hot * earlier, axis=0, keepdims=True)
    hots[0:tiles] = jnp.where((listed == place) & (rank < 1.5), 1.0, 0.0).astype(jnp.bfloat16)
    hots[tiles : 2 * tiles] = jnp.where((listed == own) & (rank > 1.5), 1.0, 0.0).astype(jnp.bfloat16)
    odd = (rank == 1.0) | (rank == 3.0)

    for l in range(levels):
        dry[l] = jnp.broadcast_to(arid[:, l : l + 1] * (-LOG2E), (gpts, 128))

    def column(row):
        return jnp.broadcast_to(row[...], (128, gpts)).T

    share_c, insol_c, matt_c = column(share), column(insol), column(matt) * (-LOG2E)
    inv_mu = 1.0 / mu[...]
    sun = mu[...] * lit[...].astype(F32)

    def advance(x, coefficient, n, s):
        east, west = pltpu.roll(x, cols - 1, 1), pltpu.roll(x, 1, 1)
        return x + coefficient * (n + s + east + west - 4.0 * x)

    def arrive(copies):
        for copy in copies:
            copy.wait_recv()

    loads[1].wait()
    loads[2].wait()
    arrive(halos)
    shared = []
    for field, whole in enumerate((q2, t2)):
        x = [halo[0, field], halo[1, field], mine[field], halo[2, field], halo[3, field]]
        x = [jnp.where((me + d >= 0) & (me + d < tiles), v, 0.0) for d, v in zip(range(-2, 3), x)]
        north = jnp.where(me > 0, advance(x[1], coefs[0], x[0], x[2]), 0.0)
        south = jnp.where(me < tiles - 1, advance(x[3], coefs[1], x[2], x[4]), 0.0)
        own_row = advance(x[2], spread[...], x[1], x[3])
        here = whole.at[pl.ds(grp * part, part)]
        here[...] = advance(own_row, spread[...], north, south).reshape(part, 1, cols)
        for k in across:
            shared.append(
                remote(here, here, xs.at[field, k], xr.at[field, k], {"grp": lax.rem(grp + k, groups)})
            )
            shared[-1].start()

    arrive(phase1)
    for k in range(ydim):
        out2a[k] = mida.reshape(tiles, 2 * SLOT)[pl.ds(k, zcdim, stride=ydim), :]
    for k in range(zdim):
        out2b[k] = midb.reshape(tiles, 2 * SLOT)[pl.ds(k, ycdim, stride=zdim), :]
    phase2 = spread_out(out2a, gota, y, at_y, p2s.at[0], p2r.at[0])
    phase2 += spread_out(out2b, gotb, z, at_z, p2s.at[1], p2r.at[1])
    gota[y] = out2a[y]
    gotb[z] = out2b[z]

    arrive(shared)
    last = (groups - 1) * part
    vapour = [
        pltpu.make_async_copy(q2.at[pl.ds(0, last)], vap_o.at[pl.ds(0, last)], vap_sem.at[0]),
        pltpu.make_async_copy(
            q2.at[pl.ds(last + gap, levels - last)], vap_o.at[pl.ds(last, levels - last)], vap_sem.at[1]
        ),
    ]
    for copy in vapour:
        copy.start()
    dts[0] = -t2[0]
    dts[1:last] = t2[0 : last - 1] - t2[1:last]
    dts[last] = t2[last - 1] - t2[last + gap]
    dts[last + 1 : levels] = t2[last + gap : levels + gap - 1] - t2[last + gap + 1 : levels + gap]
    dts[levels] = t2[levels + gap - 1]

    arrive(phase2)
    table = jnp.concatenate(
        [gota[...].reshape(tiles, 2 * SLOT), gotb[...].reshape(tiles, 2 * SLOT)], axis=0
    )
    picked = jnp.zeros((2 * SLOT, cols), F32)
    for _ in range(3):
        part = table.astype(jnp.bfloat16)
        table = table - part.astype(F32)
        picked = picked + lax.dot_general(
            part, hots[...], (((0,), (0,)), ((), ())), preferred_element_type=F32
        )
    chosen = jnp.where(odd, picked[SLOT : SLOT + gpts], picked[0:gpts])
    for half in range(cols // 128):
        wbuf[half] = chosen[:, 128 * half : 128 * half + 128] * matt_c

    reduce = []
    for half in range(cols // 128):
        lanes = pl.ds(128 * half, 128)
        w = wbuf[half]
        inv = inv_mu[:, 128 * half : 128 * half + 128]
        s0 = insol_c * sun[:, 128 * half : 128 * half + 128]

        def down(l, carry, w=w, inv=inv, lanes=lanes):
            d, s = carry
            a = dry[l] + w * q2[jnp.where(l < last, l, l + gap), :, lanes]
            t, u = jnp.exp2(a), jnp.exp2(a * inv)
            m = t * d
            tbuf[l] = t
            mbuf[l] = m
            s = s * u
            acc[l + 1] = fold8(s)
            return m + dts[l + 1, :, lanes], s

        def up(i, e, lanes=lanes):
            l = levels - 1 - i
            acc[l + 1] += fold8((mbuf[l] - e) * share_c)
            return tbuf[l] * e + dts_minus(l, lanes)

        def dts_minus(l, lanes):
            return -dts[l, :, lanes]

        start = jnp.broadcast_to(dts[0, :, lanes], (gpts, 128))
        lax.fori_loop(0, levels, down, (start, s0), unroll=10)
        e = lax.fori_loop(0, levels, up, jnp.zeros((gpts, 128), F32), unroll=10)
        acc[0] = fold8(s0 - share_c * e)
        total = acc[:, 0, :]
        for k in range(1, 8):
            total = total + acc[:, k, :]
        flux[...] = total
        gbuf[half, grp] = flux[0:levels, :] - flux[1 : levels + 1, :]
        for k in across:
            reduce.append(
                remote(
                    gbuf.at[half, grp], gbuf.at[half, grp], gs.at[half, k], gr.at[half, k],
                    {"grp": lax.rem(grp + k, groups)},
                )
            )
            reduce[-1].start()

    for half in range(cols // 128):
        for copy in reduce[half * (groups - 1) : (half + 1) * (groups - 1)]:
            copy.wait_recv()
        total = gbuf[half, 0]
        for k in range(1, groups):
            total = total + gbuf[half, k]
        lanes = pl.ds(128 * half, 128)
        total = total * (1.0 / (groups * gpts))
        total = total.reshape(levels, 1, 128)
        heat_o[:, :, lanes] = total
        temp_o[0:last, :, lanes] = t2[0:last, :, lanes] + total[0:last]
        temp_o[last:levels, :, lanes] = t2[last + gap : levels + gap, :, lanes] + total[last:levels]
    for copy in vapour:
        copy.wait()
    for copy in halos + shared + phase1 + phase2 + reduce:
        copy.wait_send()


def finish_kernel(heat, temp, vap, heat_o, temp_o, vap_o, sem):
    copies = [
        pltpu.make_async_copy(value, out, sem.at[k])
        for k, (value, out) in enumerate(((heat, heat_o), (temp, temp_o), (vap, vap_o)))
    ]
    for copy in copies:
        copy.start()
    for copy in copies:
        copy.wait()


def on_device(
    tiles, ydim, groups,
    kelvin, moisture, spread, mu, lit, owner, fac, arid, matt, share, insol,
):
    levels, _, cols = kelvin.shape
    gpts, slots = fac.shape
    zcdim, ycdim = tiles // ydim, CORES * ydim
    zdim = zcdim // CORES
    most = max(zcdim, ycdim)
    vmem, hbm = pl.BlockSpec(memory_space=pltpu.VMEM), pl.BlockSpec(memory_space=pltpu.HBM)
    dma = pltpu.SemaphoreType.DMA
    part = -(-levels // (8 * groups)) * 8
    whole = pltpu.VMEM((groups * part, 1, cols), F32)
    out = pltpu.VMEM((levels, 1, cols), F32)
    heat, temp, vap = pl.pallas_call(
        functools.partial(radiation_kernel, (tiles, ydim, groups)),
        out_shape=(out, out, out),
        in_specs=[hbm] * 11,
        out_specs=(vmem, vmem, vmem),
        scratch_shapes=[
            pltpu.VMEM((gpts, slots), F32),
            pltpu.VMEM((1, cols), F32), pltpu.VMEM((1, cols), F32), pltpu.VMEM((1, cols), jnp.int32), pltpu.VMEM((1, cols), jnp.int32),
            pltpu.VMEM((gpts, levels), F32), pltpu.VMEM((1, gpts), F32), pltpu.VMEM((1, gpts), F32), pltpu.VMEM((1, gpts), F32),
            pltpu.VMEM((slots, 128), F32),
            pltpu.VMEM((zcdim, ydim, 128), F32), pltpu.VMEM((ycdim, zdim, 128), F32),
            pltpu.VMEM((zcdim, ydim, 128), F32), pltpu.VMEM((ycdim, zdim, 128), F32),
            pltpu.VMEM((ydim, zcdim, 128), F32), pltpu.VMEM((zdim, ycdim, 128), F32),
            pltpu.VMEM((ydim, zcdim, 128), F32), pltpu.VMEM((zdim, ycdim, 128), F32),
            pltpu.VMEM((2 * tiles, cols), jnp.bfloat16),
            pltpu.VMEM((2, part, cols), F32),
            pltpu.VMEM((4, 2, part, cols), F32),
            pltpu.VMEM((2, 1, cols), F32),
            whole, whole,
            pltpu.VMEM((levels + 1, 1, cols), F32),
            pltpu.VMEM((levels, gpts, 128), F32),
            pltpu.VMEM((levels, gpts, 128), F32),
            pltpu.VMEM((levels, gpts, 128), F32),
            pltpu.VMEM((levels + 1, 8, 128), F32),
            pltpu.VMEM((levels + 1, 128), F32),
            pltpu.VMEM((cols // 128, groups, levels, 128), F32),
            pltpu.VMEM((cols // 128, gpts, 128), F32),
            dma((11,)), dma((4, 2)), dma((4, 2)), dma((2,)), dma((2,)), dma((2, groups)), dma((2, groups)), dma((2,)),
            dma((2, most)), dma((2, most)), dma((2, most)), dma((2, most)),
            dma((2, groups)), dma((2, groups)),
        ],
        compiler_params=pltpu.CompilerParams(
            collective_id=0, has_side_effects=True, vmem_limit_bytes=56 * 2**20
        ),
    )(
        kelvin, moisture, spread, mu, lit, owner.reshape(1, cols), fac, arid,
        matt.reshape(1, gpts), share.reshape(1, gpts), insol.reshape(1, gpts),
    )
    out = jax.ShapeDtypeStruct(kelvin.shape, F32)
    return pl.pallas_call(
        finish_kernel,
        out_shape=(out, out, out),
        in_specs=[vmem] * 3,
        out_specs=(hbm,) * 3,
        scratch_shapes=[dma((3,))],
        compiler_params=pltpu.CompilerParams(vmem_limit_bytes=2**20),
    )(heat, temp, vap)


def solution(mesh):
    tiles, groups = mesh.shape["tile"], mesh.shape["grp"]
    ydim = min(ROWS_Y, tiles // (2 * CORES))
    wide, row = P(None, "tile", None), P("tile", None)
    in_specs = (
        wide, wide, row, row, row, row, P("grp", "tile"), P("grp", None), P("grp"), P("grp"), P("grp"),
    )
    return jax.shard_map(
        functools.partial(on_device, tiles, ydim, groups),
        mesh=mesh,
        in_specs=in_specs,
        out_specs=(wide, wide, wide),
        check_vma=False,
    )
```

```python
import functools
import math

import jax
import jax.numpy as jnp
from jax import lax
from jax.experimental import pallas as pl
from jax.experimental.pallas import tpu as pltpu
from jax.sharding import PartitionSpec as P

F32 = jnp.float32
CORES, ROWS_Y = 2, 8
CAP = 4
SLOT = 64
MESH = pl.DeviceIdType.MESH
LOG2E = math.log2(math.e)


def remote(src, dst, send, recv, where):
    return pltpu.make_async_remote_copy(
        src_ref=src, dst_ref=dst, send_sem=send, recv_sem=recv, device_id=where, device_id_type=MESH
    )


def far_first(n):
    return sorted(range(n), key=lambda d: -min(d, n - d))


def pair(rows, base, count, step):
    low, high = (rows[pl.ds(base + r, count, stride=step), :] for r in (0, 1))
    return low + pltpu.roll(high, SLOT, 1)


def fold8(x):
    parts = [x[8 * k : 8 * k + 8] for k in range(x.shape[0] // 8)]
    while len(parts) > 1:
        parts = [sum(parts[k : k + 2][1:], parts[k]) for k in range(0, len(parts), 2)]
    return parts[0]


def radiation_kernel(
    dims,
    kel, moi, spread_h, mu_h, lit_h, owner_h, fac, arid_h, matt_h, share_h, insol_h,
    heat_o, temp_o, vap_o,
    facv, spread, mu, lit, owner, arid, matt, share, insol, fact, out1a, out1b, mida, midb, out2a, out2b, gota, gotb, hots,
    mine, halo, coefs, q2, t2, dts,
    dry, tbuf, mbuf, acc, flux, gbuf, wbuf,
    load_sem, hs, hr, cs, cr, xs, xr, vap_sem, p1s, p1r, p2s, p2r, gs, gr,
):
    tiles, ydim, groups = dims
    zcdim, ycdim = tiles // ydim, CORES * ydim
    levels, _, cols = kel.shape
    part = halo.shape[2]
    gap = groups * part - levels
    gpts = arid.shape[0]
    me, grp = lax.axis_index("tile"), lax.axis_index("grp")
    core, y, z = lax.rem(me, CORES), lax.rem(me // CORES, ydim), me // (CORES * ydim)
    zdim = zcdim // CORES
    zc, yc = z * CORES + core, y * CORES + core

    def tile_of(a, b, c):
        return (a * ydim + b) * CORES + c

    near = [(d, c) for d in far_first(zdim) for c in (1, 0) if d or c]
    at_zc = []
    for d, c in near:
        zz, cc = lax.rem(z + d, zdim), lax.rem(core + c, CORES)
        at_zc.append((tile_of(zz, y, cc), zz * CORES + cc))
    at_yc = []
    for d, c in [(d, c) for d in far_first(ydim) for c in (1, 0) if d or c]:
        yy, cc = lax.rem(y + d, ydim), lax.rem(core + c, CORES)
        at_yc.append((tile_of(z, yy, cc), yy * CORES + cc))
    at_y = [(tile_of(z, lax.rem(y + d, ydim), core), lax.rem(y + d, ydim)) for d in far_first(ydim) if d]
    at_z = [(tile_of(lax.rem(z + d, zdim), y, core), lax.rem(z + d, zdim)) for d in far_first(zdim) if d]
    across = [k for k in far_first(groups) if k]

    rows = [(lax.rem(me + tiles - d, tiles), k) for k, d in enumerate((-2, -1, 1, 2))]
    level = jnp.minimum(grp * part, levels - part)

    peers = [{"tile": where} for where, _ in rows]
    peers += [{"tile": where} for where, _ in at_zc] + [{"tile": where} for where, _ in at_yc]
    peers += [{"grp": lax.rem(grp + k, groups)} for k in across]
    loads = [
        pltpu.make_async_copy(src, dst, load_sem.at[k])
        for k, (src, dst) in enumerate(
            (
                (fac, facv), (moi.at[pl.ds(level, part), 0, :], mine.at[0]), (kel.at[pl.ds(level, part), 0, :], mine.at[1]),
                (owner_h, owner), (arid_h, arid), (matt_h, matt), (share_h, share), (insol_h, insol), (mu_h, mu),
                (lit_h, lit), (spread_h, spread),
            )
        )
    ]
    for load in loads:
        load.start()

    barrier = pltpu.get_barrier_semaphore()
    for peer in peers:
        pl.semaphore_signal(barrier, inc=1, device_id=peer, device_id_type=MESH)

    loads[0].wait()
    tall = jnp.concatenate([facv[...], jnp.zeros((128 - gpts, facv.shape[1]), F32)], axis=0)
    fact[...] = tall.T
    step = CORES * CAP
    for k in range(zcdim):
        base = (k // CORES) * (ydim * step) + (k % CORES) * CAP
        out1a[k] = pair(fact, base, ydim, step)
    for k in range(ycdim):
        out1b[k] = pair(fact, k * CAP + 2, zdim, ydim * step)

    pl.semaphore_wait(barrier, len(peers))

    def spread_out(source, target, mine, partners, send, recv):
        copies = []
        for k, (where, other) in enumerate(partners):
            copies.append(
                remote(source.at[other], target.at[mine], send.at[k], recv.at[k], {"tile": where})
            )
            copies[-1].start()
        return copies

    phase1 = spread_out(out1a, mida, zc, at_zc, p1s.at[0], p1r.at[0])
    phase1 += spread_out(out1b, midb, yc, at_yc, p1s.at[1], p1r.at[1])
    halos = []
    for where, k in rows:
        for field, source in enumerate((moi, kel)):
            halos.append(
                remote(
                    source.at[pl.ds(level, part), 0, :], halo.at[k, field], hs.at[k, field], hr.at[k, field],
                    {"tile": where},
                )
            )
        if k in (1, 2):
            halos.append(remote(spread_h, coefs.at[k - 1], cs.at[k - 1], cr.at[k - 1], {"tile": where}))
    for copy in halos:
        copy.start()

    mida[zc] = out1a[zc]
    midb[yc] = out1b[yc]

    for load in loads[3:]:
        load.wait()
    own = owner[...]
    place = lax.rem(own // CORES, ydim) * zcdim + (own // ycdim) * CORES + lax.rem(own, CORES)
    listed = lax.broadcasted_iota(jnp.int32, (tiles, cols), 0)
    hot = jnp.where(listed == own, 1.0, 0.0)
    before = jnp.where(
        lax.broadcasted_iota(jnp.int32, (cols, cols), 0) < lax.broadcasted_iota(jnp.int32, (cols, cols), 1),
        1.0,
        0.0,
    )
    earlier = jnp.dot(hot.astype(jnp.bfloat16), before.astype(jnp.bfloat16), preferred_element_type=F32)
    rank = jnp.sum(hot * earlier, axis=0, keepdims=True)
    hots[0:tiles] = jnp.where((listed == place) & (rank < 1.5), 1.0, 0.0).astype(jnp.bfloat16)
    hots[tiles : 2 * tiles] = jnp.where((listed == own) & (rank > 1.5), 1.0, 0.0).astype(jnp.bfloat16)
    odd = (rank == 1.0) | (rank == 3.0)

    for l in range(levels):
        dry[l] = jnp.broadcast_to(arid[:, l : l + 1] * (-LOG2E), (gpts, 128))

    def column(row):
        return jnp.broadcast_to(row[...], (128, gpts)).T

    share_c, insol_c, matt_c = column(share), column(insol), column(matt) * (-LOG2E)
    inv_mu = 1.0 / mu[...]
    sun = mu[...] * lit[...].astype(F32)

    def advance(x, coefficient, n, s):
        east, west = pltpu.roll(x, cols - 1, 1), pltpu.roll(x, 1, 1)
        return x + coefficient * (n + s + east + west - 4.0 * x)

    def arrive(copies):
        for copy in copies:
            copy.wait_recv()

    loads[1].wait()
    loads[2].wait()
    arrive(halos)
    shared = []
    for field, whole in enumerate((q2, t2)):
        x = [halo[0, field], halo[1, field], mine[field], halo[2, field], halo[3, field]]
        x = [jnp.where((me + d >= 0) & (me + d < tiles), v, 0.0) for d, v in zip(range(-2, 3), x)]
        north = jnp.where(me > 0, advance(x[1], coefs[0], x[0], x[2]), 0.0)
        south = jnp.where(me < tiles - 1, advance(x[3], coefs[1], x[2], x[4]), 0.0)
        own_row = advance(x[2], spread[...], x[1], x[3])
        here = whole.at[pl.ds(grp * part, part)]
        here[...] = advance(own_row, spread[...], north, south).reshape(part, 1, cols)
        for k in across:
            shared.append(
                remote(here, here, xs.at[field, k], xr.at[field, k], {"grp": lax.rem(grp + k, groups)})
            )
            shared[-1].start()

    arrive(phase1)
    for k in range(ydim):
        out2a[k] = mida.reshape(tiles, 2 * SLOT)[pl.ds(k, zcdim, stride=ydim), :]
    for k in range(zdim):
        out2b[k] = midb.reshape(tiles, 2 * SLOT)[pl.ds(k, ycdim, stride=zdim), :]
    phase2 = spread_out(out2a, gota, y, at_y, p2s.at[0], p2r.at[0])
    phase2 += spread_out(out2b, gotb, z, at_z, p2s.at[1], p2r.at[1])
    gota[y] = out2a[y]
    gotb[z] = out2b[z]

    arrive(shared)
    last = (groups - 1) * part
    vapour = [
        pltpu.make_async_copy(q2.at[pl.ds(0, last)], vap_o.at[pl.ds(0, last)], vap_sem.at[0]),
        pltpu.make_async_copy(
            q2.at[pl.ds(last + gap, levels - last)], vap_o.at[pl.ds(last, levels - last)], vap_sem.at[1]
        ),
    ]
    for copy in vapour:
        copy.start()
    dts[0] = -t2[0]
    dts[1:last] = t2[0 : last - 1] - t2[1:last]
    dts[last] = t2[last - 1] - t2[last + gap]
    dts[last + 1 : levels] = t2[last + gap : levels + gap - 1] - t2[last + gap + 1 : levels + gap]
    dts[levels] = t2[levels + gap - 1]

    arrive(phase2)
    table = jnp.concatenate(
        [gota[...].reshape(tiles, 2 * SLOT), gotb[...].reshape(tiles, 2 * SLOT)], axis=0
    )
    picked = jnp.zeros((2 * SLOT, cols), F32)
    for _ in range(3):
        part = table.astype(jnp.bfloat16)
        table = table - part.astype(F32)
        picked = picked + lax.dot_general(
            part, hots[...], (((0,), (0,)), ((), ())), preferred_element_type=F32
        )
    chosen = jnp.where(odd, picked[SLOT : SLOT + gpts], picked[0:gpts])
    for half in range(cols // 128):
        wbuf[half] = chosen[:, 128 * half : 128 * half + 128] * matt_c

    ratio = insol_c / share_c
    folded = acc.reshape(8 * (levels + 1), 128)
    reduce = []
    for half in range(cols // 128):
        lanes = pl.ds(128 * half, 128)
        w = wbuf[half]
        inv = inv_mu[:, 128 * half : 128 * half + 128]
        s0 = ratio * sun[:, 128 * half : 128 * half + 128]

        def down(l, carry, w=w, inv=inv, lanes=lanes):
            d, s = carry
            a = dry[l] + w * q2[jnp.where(l < last, l, l + gap), :, lanes]
            t, u = jnp.exp2(a), jnp.exp2(a * inv)
            m = t * d
            s = s * u
            tbuf[l] = t
            mbuf[l] = m + s
            return m + dts[l + 1, :, lanes], s

        def up(i, e, lanes=lanes):
            l = levels - 1 - i
            acc[l + 1] = fold8((mbuf[l] - e) * share_c)
            return tbuf[l] * e + dts_minus(l, lanes)

        def dts_minus(l, lanes):
            return -dts[l, :, lanes]

        start = jnp.broadcast_to(dts[0, :, lanes], (gpts, 128))
        lax.fori_loop(0, levels, down, (start, s0), unroll=10)
        e = lax.fori_loop(0, levels, up, jnp.zeros((gpts, 128), F32), unroll=10)
        acc[0] = fold8((s0 - e) * share_c)
        total = folded[pl.ds(0, levels + 1, stride=8), :]
        for k in range(1, 8):
            total = total + folded[pl.ds(k, levels + 1, stride=8), :]
        flux[...] = total
        gbuf[half, grp] = flux[0:levels, :] - flux[1 : levels + 1, :]
        for k in across:
            reduce.append(
                remote(
                    gbuf.at[half, grp], gbuf.at[half, grp], gs.at[half, k], gr.at[half, k],
                    {"grp": lax.rem(grp + k, groups)},
                )
            )
            reduce[-1].start()

    for copy in vapour:
        copy.wait()
    for copy in halos + shared + phase1 + phase2:
        copy.wait_send()
    for half in range(cols // 128):
        for copy in reduce[half * (groups - 1) : (half + 1) * (groups - 1)]:
            copy.wait_recv()
        total = gbuf[half, 0]
        for k in range(1, groups):
            total = total + gbuf[half, k]
        lanes = pl.ds(128 * half, 128)
        total = total * (1.0 / (groups * gpts))
        total = total.reshape(levels, 1, 128)
        heat_o[:, :, lanes] = total
        temp_o[0:last, :, lanes] = t2[0:last, :, lanes] + total[0:last]
        temp_o[last:levels, :, lanes] = t2[last + gap : levels + gap, :, lanes] + total[last:levels]
    for copy in reduce:
        copy.wait_send()


def finish_kernel(heat, temp, vap, heat_o, temp_o, vap_o, sem):
    copies = [
        pltpu.make_async_copy(value, out, sem.at[k])
        for k, (value, out) in enumerate(((heat, heat_o), (temp, temp_o), (vap, vap_o)))
    ]
    for copy in copies:
        copy.start()
    for copy in copies:
        copy.wait()


def on_device(
    tiles, ydim, groups,
    kelvin, moisture, spread, mu, lit, owner, fac, arid, matt, share, insol,
):
    levels, _, cols = kelvin.shape
    gpts, slots = fac.shape
    zcdim, ycdim = tiles // ydim, CORES * ydim
    zdim = zcdim // CORES
    most = max(zcdim, ycdim)
    vmem, hbm = pl.BlockSpec(memory_space=pltpu.VMEM), pl.BlockSpec(memory_space=pltpu.HBM)
    dma = pltpu.SemaphoreType.DMA
    part = -(-levels // (8 * groups)) * 8
    whole = pltpu.VMEM((groups * part, 1, cols), F32)
    out = pltpu.VMEM((levels, 1, cols), F32)
    heat, temp, vap = pl.pallas_call(
        functools.partial(radiation_kernel, (tiles, ydim, groups)),
        out_shape=(out, out, out),
        in_specs=[hbm] * 11,
        out_specs=(vmem, vmem, vmem),
        scratch_shapes=[
            pltpu.VMEM((gpts, slots), F32),
            pltpu.VMEM((1, cols), F32), pltpu.VMEM((1, cols), F32), pltpu.VMEM((1, cols), jnp.int32), pltpu.VMEM((1, cols), jnp.int32),
            pltpu.VMEM((gpts, levels), F32), pltpu.VMEM((1, gpts), F32), pltpu.VMEM((1, gpts), F32), pltpu.VMEM((1, gpts), F32),
            pltpu.VMEM((slots, 128), F32),
            pltpu.VMEM((zcdim, ydim, 128), F32), pltpu.VMEM((ycdim, zdim, 128), F32),
            pltpu.VMEM((zcdim, ydim, 128), F32), pltpu.VMEM((ycdim, zdim, 128), F32),
            pltpu.VMEM((ydim, zcdim, 128), F32), pltpu.VMEM((zdim, ycdim, 128), F32),
            pltpu.VMEM((ydim, zcdim, 128), F32), pltpu.VMEM((zdim, ycdim, 128), F32),
            pltpu.VMEM((2 * tiles, cols), jnp.bfloat16),
            pltpu.VMEM((2, part, cols), F32),
            pltpu.VMEM((4, 2, part, cols), F32),
            pltpu.VMEM((2, 1, cols), F32),
            whole, whole,
            pltpu.VMEM((levels + 1, 1, cols), F32),
            pltpu.VMEM((levels, gpts, 128), F32),
            pltpu.VMEM((levels, gpts, 128), F32),
            pltpu.VMEM((levels, gpts, 128), F32),
            pltpu.VMEM((levels + 1, 8, 128), F32),
            pltpu.VMEM((levels + 1, 128), F32),
            pltpu.VMEM((cols // 128, groups, levels, 128), F32),
            pltpu.VMEM((cols // 128, gpts, 128), F32),
            dma((11,)), dma((4, 2)), dma((4, 2)), dma((2,)), dma((2,)), dma((2, groups)), dma((2, groups)), dma((2,)),
            dma((2, most)), dma((2, most)), dma((2, most)), dma((2, most)),
            dma((2, groups)), dma((2, groups)),
        ],
        compiler_params=pltpu.CompilerParams(
            collective_id=0, has_side_effects=True, vmem_limit_bytes=56 * 2**20
        ),
    )(
        kelvin, moisture, spread, mu, lit, owner.reshape(1, cols), fac, arid,
        matt.reshape(1, gpts), share.reshape(1, gpts), insol.reshape(1, gpts),
    )
    out = jax.ShapeDtypeStruct(kelvin.shape, F32)
    return pl.pallas_call(
        finish_kernel,
        out_shape=(out, out, out),
        in_specs=[vmem] * 3,
        out_specs=(hbm,) * 3,
        scratch_shapes=[dma((3,))],
        compiler_params=pltpu.CompilerParams(vmem_limit_bytes=2**20),
    )(heat, temp, vap)


def solution(mesh):
    tiles, groups = mesh.shape["tile"], mesh.shape["grp"]
    ydim = min(ROWS_Y, tiles // (2 * CORES))
    wide, row = P(None, "tile", None), P("tile", None)
    in_specs = (
        wide, wide, row, row, row, row, P("grp", "tile"), P("grp", None), P("grp"), P("grp"), P("grp"),
    )
    return jax.shard_map(
        functools.partial(on_device, tiles, ydim, groups),
        mesh=mesh,
        in_specs=in_specs,
        out_specs=(wide, wide, wide),
        check_vma=False,
    )
```

```python
import functools
import math

import jax
import jax.numpy as jnp
from jax import lax
from jax.experimental import pallas as pl
from jax.experimental.pallas import tpu as pltpu
from jax.sharding import PartitionSpec as P

F32 = jnp.float32
CORES, ROWS_Y = 2, 8
CAP = 4
SLOT = 64
MESH = pl.DeviceIdType.MESH
LOG2E = math.log2(math.e)


def remote(src, dst, send, recv, where):
    return pltpu.make_async_remote_copy(
        src_ref=src, dst_ref=dst, send_sem=send, recv_sem=recv, device_id=where, device_id_type=MESH
    )


def far_first(n):
    return sorted(range(n), key=lambda d: -min(d, n - d))


def pair(rows, base, count, step):
    low, high = (rows[pl.ds(base + r, count, stride=step), :] for r in (0, 1))
    return low + pltpu.roll(high, SLOT, 1)


def fold8(x):
    parts = [x[8 * k : 8 * k + 8] for k in range(x.shape[0] // 8)]
    while len(parts) > 1:
        parts = [sum(parts[k : k + 2][1:], parts[k]) for k in range(0, len(parts), 2)]
    return parts[0]


def radiation_kernel(
    dims,
    kel, moi, spread_h, mu_h, lit_h, owner_h, fac, arid_h, matt_h, share_h, insol_h,
    heat_o, temp_o, vap_o,
    facv, spread, mu, lit, owner, arid, matt, share, insol, fact, out1a, out1b, mida, midb, out2a, out2b, gota, gotb, hots,
    mine, halo, coefs, q2, t2, dts,
    dry, tbuf, mbuf, acc, flux, gbuf, wbuf,
    load_sem, hs, hr, xs, xr, vap_sem, p1s, p1r, p2s, p2r, gs, gr,
):
    tiles, ydim, groups = dims
    zcdim, ycdim = tiles // ydim, CORES * ydim
    levels, _, cols = kel.shape
    part = halo.shape[2]
    gap = groups * part - levels
    gpts = arid.shape[0]
    me, grp = lax.axis_index("tile"), lax.axis_index("grp")
    core, y, z = lax.rem(me, CORES), lax.rem(me // CORES, ydim), me // (CORES * ydim)
    zdim = zcdim // CORES
    zc, yc = z * CORES + core, y * CORES + core

    def tile_of(a, b, c):
        return (a * ydim + b) * CORES + c

    near = [(d, c) for d in far_first(zdim) for c in (1, 0) if d or c]
    at_zc = []
    for d, c in near:
        zz, cc = lax.rem(z + d, zdim), lax.rem(core + c, CORES)
        at_zc.append((tile_of(zz, y, cc), zz * CORES + cc))
    at_yc = []
    for d, c in [(d, c) for d in far_first(ydim) for c in (1, 0) if d or c]:
        yy, cc = lax.rem(y + d, ydim), lax.rem(core + c, CORES)
        at_yc.append((tile_of(z, yy, cc), yy * CORES + cc))
    at_y = [(tile_of(z, lax.rem(y + d, ydim), core), lax.rem(y + d, ydim)) for d in far_first(ydim) if d]
    at_z = [(tile_of(lax.rem(z + d, zdim), y, core), lax.rem(z + d, zdim)) for d in far_first(zdim) if d]
    across = [k for k in far_first(groups) if k]

    rows = [(lax.rem(me + tiles - d, tiles), k) for k, d in enumerate((-2, -1, 1, 2))]
    level = jnp.minimum(grp * part, levels - part)

    peers = [{"tile": where} for where, _ in rows]
    peers += [{"tile": where} for where, _ in at_zc] + [{"tile": where} for where, _ in at_yc]
    peers += [{"grp": lax.rem(grp + k, groups)} for k in across]
    loads = [
        pltpu.make_async_copy(src, dst, load_sem.at[k])
        for k, (src, dst) in enumerate(
            (
                (fac, facv), (moi.at[pl.ds(level, part), 0, :], mine.at[0]), (kel.at[pl.ds(level, part), 0, :], mine.at[1]),
                (owner_h, owner), (arid_h, arid), (matt_h, matt), (share_h, share), (insol_h, insol), (mu_h, mu),
                (lit_h, lit), (spread_h, spread),
            )
        )
    ]
    for load in loads:
        load.start()

    barrier = pltpu.get_barrier_semaphore()
    for peer in peers:
        pl.semaphore_signal(barrier, inc=1, device_id=peer, device_id_type=MESH)

    loads[0].wait()
    tall = jnp.concatenate([facv[...], jnp.zeros((128 - gpts, facv.shape[1]), F32)], axis=0)
    fact[...] = tall.T
    step = CORES * CAP
    for k in range(zcdim):
        base = (k // CORES) * (ydim * step) + (k % CORES) * CAP
        out1a[k] = pair(fact, base, ydim, step)
    for k in range(ycdim):
        out1b[k] = pair(fact, k * CAP + 2, zdim, ydim * step)

    pl.semaphore_wait(barrier, len(peers))

    def spread_out(source, target, mine, partners, send, recv):
        copies = []
        for k, (where, other) in enumerate(partners):
            copies.append(
                remote(source.at[other], target.at[mine], send, recv, {"tile": where})
            )
            copies[-1].start()
        all_but_one = pl.ds(0, len(partners))
        return [remote(source.at[all_but_one], target.at[all_but_one], send, recv, {"tile": partners[0][0]})]

    phase1 = spread_out(out1a, mida, zc, at_zc, p1s.at[0], p1r.at[0])
    phase1 += spread_out(out1b, midb, yc, at_yc, p1s.at[1], p1r.at[1])
    halos = []
    for where, k in rows:
        for field, source in enumerate((moi, kel)):
            halos.append(
                remote(
                    source.at[pl.ds(level, part), 0, :], halo.at[k, field], hs.at[0], hr.at[0],
                    {"tile": where},
                )
            )
        if k in (1, 2):
            halos.append(remote(spread_h, coefs.at[k - 1], hs.at[1], hr.at[1], {"tile": where}))
    for copy in halos:
        copy.start()
    nearby = {"tile": rows[0][0]}
    halos = [
        remote(halo, halo, hs.at[0], hr.at[0], nearby),
        remote(coefs, coefs, hs.at[1], hr.at[1], nearby),
    ]

    mida[zc] = out1a[zc]
    midb[yc] = out1b[yc]

    for load in loads[3:]:
        load.wait()
    own = owner[...]
    place = lax.rem(own // CORES, ydim) * zcdim + (own // ycdim) * CORES + lax.rem(own, CORES)
    listed = lax.broadcasted_iota(jnp.int32, (tiles, cols), 0)
    hot = jnp.where(listed == own, 1.0, 0.0)
    before = jnp.where(
        lax.broadcasted_iota(jnp.int32, (cols, cols), 0) < lax.broadcasted_iota(jnp.int32, (cols, cols), 1),
        1.0,
        0.0,
    )
    earlier = jnp.dot(hot.astype(jnp.bfloat16), before.astype(jnp.bfloat16), preferred_element_type=F32)
    rank = jnp.sum(hot * earlier, axis=0, keepdims=True)
    hots[0:tiles] = jnp.where((listed == place) & (rank < 1.5), 1.0, 0.0).astype(jnp.bfloat16)
    hots[tiles : 2 * tiles] = jnp.where((listed == own) & (rank > 1.5), 1.0, 0.0).astype(jnp.bfloat16)
    odd = (rank == 1.0) | (rank == 3.0)

    for l in range(levels):
        dry[l] = jnp.broadcast_to(arid[:, l : l + 1] * (-LOG2E), (gpts, 128))

    def column(row):
        return jnp.broadcast_to(row[...], (128, gpts)).T

    share_c, insol_c, matt_c = column(share), column(insol), column(matt) * (-LOG2E)
    inv_mu = 1.0 / mu[...]
    sun = mu[...] * lit[...].astype(F32)

    def advance(x, coefficient, n, s):
        east, west = pltpu.roll(x, cols - 1, 1), pltpu.roll(x, 1, 1)
        return x + coefficient * (n + s + east + west - 4.0 * x)

    def arrive(copies):
        for copy in copies:
            copy.wait_recv()

    arrive(phase1)
    for k in range(ydim):
        out2a[k] = mida.reshape(tiles, 2 * SLOT)[pl.ds(k, zcdim, stride=ydim), :]
    for k in range(zdim):
        out2b[k] = midb.reshape(tiles, 2 * SLOT)[pl.ds(k, ycdim, stride=zdim), :]
    phase2 = spread_out(out2a, gota, y, at_y, p2s.at[0], p2r.at[0])
    phase2 += spread_out(out2b, gotb, z, at_z, p2s.at[1], p2r.at[1])
    gota[y] = out2a[y]
    gotb[z] = out2b[z]

    loads[1].wait()
    loads[2].wait()
    arrive(halos)
    shared = []
    for field, whole in enumerate((q2, t2)):
        x = [halo[0, field], halo[1, field], mine[field], halo[2, field], halo[3, field]]
        x = [jnp.where((me + d >= 0) & (me + d < tiles), v, 0.0) for d, v in zip(range(-2, 3), x)]
        north = jnp.where(me > 0, advance(x[1], coefs[0], x[0], x[2]), 0.0)
        south = jnp.where(me < tiles - 1, advance(x[3], coefs[1], x[2], x[4]), 0.0)
        own_row = advance(x[2], spread[...], x[1], x[3])
        here = whole.at[pl.ds(grp * part, part)]
        here[...] = advance(own_row, spread[...], north, south).reshape(part, 1, cols)
        for k in across:
            remote(here, here, xs.at[field], xr.at[field], {"grp": lax.rem(grp + k, groups)}).start()
        others = whole.at[pl.ds(0, (groups - 1) * part)]
        shared.append(
            remote(others, others, xs.at[field], xr.at[field], {"grp": lax.rem(grp + 1, groups)})
        )

    arrive(shared)
    last = (groups - 1) * part
    vapour = [
        pltpu.make_async_copy(q2.at[pl.ds(0, last)], vap_o.at[pl.ds(0, last)], vap_sem.at[0]),
        pltpu.make_async_copy(
            q2.at[pl.ds(last + gap, levels - last)], vap_o.at[pl.ds(last, levels - last)], vap_sem.at[1]
        ),
    ]
    for copy in vapour:
        copy.start()
    dts[0] = -t2[0]
    dts[1:last] = t2[0 : last - 1] - t2[1:last]
    dts[last] = t2[last - 1] - t2[last + gap]
    dts[last + 1 : levels] = t2[last + gap : levels + gap - 1] - t2[last + gap + 1 : levels + gap]
    dts[levels] = t2[levels + gap - 1]

    arrive(phase2)
    table = jnp.concatenate(
        [gota[...].reshape(tiles, 2 * SLOT), gotb[...].reshape(tiles, 2 * SLOT)], axis=0
    )
    picked = jnp.zeros((2 * SLOT, cols), F32)
    for _ in range(3):
        part = table.astype(jnp.bfloat16)
        table = table - part.astype(F32)
        picked = picked + lax.dot_general(
            part, hots[...], (((0,), (0,)), ((), ())), preferred_element_type=F32
        )
    chosen = jnp.where(odd, picked[SLOT : SLOT + gpts], picked[0:gpts])
    for half in range(cols // 128):
        wbuf[half] = chosen[:, 128 * half : 128 * half + 128] * matt_c

    ratio = insol_c / share_c
    folded = acc.reshape(8 * (levels + 1), 128)
    reduce = []
    for half in range(cols // 128):
        lanes = pl.ds(128 * half, 128)
        w = wbuf[half]
        inv = inv_mu[:, 128 * half : 128 * half + 128]
        s0 = ratio * sun[:, 128 * half : 128 * half + 128]

        def down(l, carry, w=w, inv=inv, lanes=lanes):
            d, s = carry
            a = dry[l] + w * q2[jnp.where(l < last, l, l + gap), :, lanes]
            t, u = jnp.exp2(a), jnp.exp2(a * inv)
            m = t * d
            s = s * u
            tbuf[l] = t
            mbuf[l] = m + s
            return m + dts[l + 1, :, lanes], s

        def up(i, e, lanes=lanes):
            l = levels - 1 - i
            acc[l + 1] = fold8((mbuf[l] - e) * share_c)
            return tbuf[l] * e + dts_minus(l, lanes)

        def dts_minus(l, lanes):
            return -dts[l, :, lanes]

        start = jnp.broadcast_to(dts[0, :, lanes], (gpts, 128))
        lax.fori_loop(0, levels, down, (start, s0), unroll=10)
        e = lax.fori_loop(0, levels, up, jnp.zeros((gpts, 128), F32), unroll=10)
        acc[0] = fold8((s0 - e) * share_c)
        total = folded[pl.ds(0, levels + 1, stride=8), :]
        for k in range(1, 8):
            total = total + folded[pl.ds(k, levels + 1, stride=8), :]
        flux[...] = total
        gbuf[half, grp] = flux[0:levels, :] - flux[1 : levels + 1, :]
        for k in across:
            remote(
                gbuf.at[half, grp], gbuf.at[half, grp], gs.at[half], gr.at[half],
                {"grp": lax.rem(grp + k, groups)},
            ).start()
        others = gbuf.at[half, pl.ds(0, groups - 1)]
        reduce.append(
            remote(others, others, gs.at[half], gr.at[half], {"grp": lax.rem(grp + 1, groups)})
        )

    for copy in vapour:
        copy.wait()
    for copy in halos + shared + phase1 + phase2:
        copy.wait_send()
    for half in range(cols // 128):
        reduce[half].wait_recv()
        total = gbuf[half, 0]
        for k in range(1, groups):
            total = total + gbuf[half, k]
        lanes = pl.ds(128 * half, 128)
        total = total * (1.0 / (groups * gpts))
        total = total.reshape(levels, 1, 128)
        heat_o[:, :, lanes] = total
        temp_o[0:last, :, lanes] = t2[0:last, :, lanes] + total[0:last]
        temp_o[last:levels, :, lanes] = t2[last + gap : levels + gap, :, lanes] + total[last:levels]
    for copy in reduce:
        copy.wait_send()


def finish_kernel(heat, temp, vap, heat_o, temp_o, vap_o, sem):
    copies = [
        pltpu.make_async_copy(value, out, sem.at[k])
        for k, (value, out) in enumerate(((heat, heat_o), (temp, temp_o), (vap, vap_o)))
    ]
    for copy in copies:
        copy.start()
    for copy in copies:
        copy.wait()


def on_device(
    tiles, ydim, groups,
    kelvin, moisture, spread, mu, lit, owner, fac, arid, matt, share, insol,
):
    levels, _, cols = kelvin.shape
    gpts, slots = fac.shape
    zcdim, ycdim = tiles // ydim, CORES * ydim
    zdim = zcdim // CORES
    vmem, hbm = pl.BlockSpec(memory_space=pltpu.VMEM), pl.BlockSpec(memory_space=pltpu.HBM)
    dma = pltpu.SemaphoreType.DMA
    part = -(-levels // (8 * groups)) * 8
    whole = pltpu.VMEM((groups * part, 1, cols), F32)
    out = pltpu.VMEM((levels, 1, cols), F32)
    heat, temp, vap = pl.pallas_call(
        functools.partial(radiation_kernel, (tiles, ydim, groups)),
        out_shape=(out, out, out),
        in_specs=[hbm] * 11,
        out_specs=(vmem, vmem, vmem),
        scratch_shapes=[
            pltpu.VMEM((gpts, slots), F32),
            pltpu.VMEM((1, cols), F32), pltpu.VMEM((1, cols), F32), pltpu.VMEM((1, cols), jnp.int32), pltpu.VMEM((1, cols), jnp.int32),
            pltpu.VMEM((gpts, levels), F32), pltpu.VMEM((1, gpts), F32), pltpu.VMEM((1, gpts), F32), pltpu.VMEM((1, gpts), F32),
            pltpu.VMEM((slots, 128), F32),
            pltpu.VMEM((zcdim, ydim, 128), F32), pltpu.VMEM((ycdim, zdim, 128), F32),
            pltpu.VMEM((zcdim, ydim, 128), F32), pltpu.VMEM((ycdim, zdim, 128), F32),
            pltpu.VMEM((ydim, zcdim, 128), F32), pltpu.VMEM((zdim, ycdim, 128), F32),
            pltpu.VMEM((ydim, zcdim, 128), F32), pltpu.VMEM((zdim, ycdim, 128), F32),
            pltpu.VMEM((2 * tiles, cols), jnp.bfloat16),
            pltpu.VMEM((2, part, cols), F32),
            pltpu.VMEM((4, 2, part, cols), F32),
            pltpu.VMEM((2, 1, cols), F32),
            whole, whole,
            pltpu.VMEM((levels + 1, 1, cols), F32),
            pltpu.VMEM((levels, gpts, 128), F32),
            pltpu.VMEM((levels, gpts, 128), F32),
            pltpu.VMEM((levels, gpts, 128), F32),
            pltpu.VMEM((levels + 1, 8, 128), F32),
            pltpu.VMEM((levels + 1, 128), F32),
            pltpu.VMEM((cols // 128, groups, levels, 128), F32),
            pltpu.VMEM((cols // 128, gpts, 128), F32),
            dma((11,)), dma((2,)), dma((2,)), dma((2,)), dma((2,)), dma((2,)),
            dma((2,)), dma((2,)), dma((2,)), dma((2,)),
            dma((cols // 128,)), dma((cols // 128,)),
        ],
        compiler_params=pltpu.CompilerParams(
            collective_id=0, has_side_effects=True, vmem_limit_bytes=56 * 2**20
        ),
    )(
        kelvin, moisture, spread, mu, lit, owner.reshape(1, cols), fac, arid,
        matt.reshape(1, gpts), share.reshape(1, gpts), insol.reshape(1, gpts),
    )
    out = jax.ShapeDtypeStruct(kelvin.shape, F32)
    return pl.pallas_call(
        finish_kernel,
        out_shape=(out, out, out),
        in_specs=[vmem] * 3,
        out_specs=(hbm,) * 3,
        scratch_shapes=[dma((3,))],
        compiler_params=pltpu.CompilerParams(vmem_limit_bytes=2**20),
    )(heat, temp, vap)


def solution(mesh):
    tiles, groups = mesh.shape["tile"], mesh.shape["grp"]
    ydim = min(ROWS_Y, tiles // (2 * CORES))
    wide, row = P(None, "tile", None), P("tile", None)
    in_specs = (
        wide, wide, row, row, row, row, P("grp", "tile"), P("grp", None), P("grp"), P("grp"), P("grp"),
    )
    return jax.shard_map(
        functools.partial(on_device, tiles, ydim, groups),
        mesh=mesh,
        in_specs=in_specs,
        out_specs=(wide, wide, wide),
        check_vma=False,
    )
```

```python
import functools
import math

import jax
import jax.numpy as jnp
from jax import lax
from jax.experimental import pallas as pl
from jax.experimental.pallas import tpu as pltpu
from jax.sharding import PartitionSpec as P

F32 = jnp.float32
CORES, ROWS_Y = 2, 8
CAP = 4
SLOT = 64
MESH = pl.DeviceIdType.MESH
LOG2E = math.log2(math.e)


def remote(src, dst, send, recv, where):
    return pltpu.make_async_remote_copy(
        src_ref=src, dst_ref=dst, send_sem=send, recv_sem=recv, device_id=where, device_id_type=MESH
    )


def far_first(n):
    return sorted(range(n), key=lambda d: -min(d, n - d))


def pair(rows, base, count, step):
    low, high = (rows[pl.ds(base + r, count, stride=step), :] for r in (0, 1))
    return low + pltpu.roll(high, SLOT, 1)


def fold8(x):
    parts = [x[8 * k : 8 * k + 8] for k in range(x.shape[0] // 8)]
    while len(parts) > 1:
        parts = [sum(parts[k : k + 2][1:], parts[k]) for k in range(0, len(parts), 2)]
    return parts[0]


def radiation_kernel(
    dims,
    kel, moi, spread_h, mu_h, lit_h, owner_h, fac, arid_h, matt_h, share_h, insol_h,
    heat_o, temp_o, vap_o,
    facv, spread, mu, lit, owner, arid, matt, share, insol, fact, out1a, out1b, mida, midb, out2a, out2b, gota, gotb, hots,
    mine, halo, coefs, q2, t2, dts,
    dry, tbuf, mbuf, acc, flux, gbuf, wbuf,
    load_sem, hs, hr, xs, xr, vap_sem, p1s, p1r, p2s, p2r, gs, gr,
):
    tiles, ydim, groups = dims
    zcdim, ycdim = tiles // ydim, CORES * ydim
    levels, _, cols = kel.shape
    part = halo.shape[2]
    gap = groups * part - levels
    gpts = arid.shape[0]
    me, grp = lax.axis_index("tile"), lax.axis_index("grp")
    core, y, z = lax.rem(me, CORES), lax.rem(me // CORES, ydim), me // (CORES * ydim)
    zdim = zcdim // CORES
    zc, yc = z * CORES + core, y * CORES + core

    def tile_of(a, b, c):
        return (a * ydim + b) * CORES + c

    near = [(d, c) for d in far_first(zdim) for c in (1, 0) if d or c]
    at_zc = []
    for d, c in near:
        zz, cc = lax.rem(z + d, zdim), lax.rem(core + c, CORES)
        at_zc.append((tile_of(zz, y, cc), zz * CORES + cc))
    at_yc = []
    for d, c in [(d, c) for d in far_first(ydim) for c in (1, 0) if d or c]:
        yy, cc = lax.rem(y + d, ydim), lax.rem(core + c, CORES)
        at_yc.append((tile_of(z, yy, cc), yy * CORES + cc))
    at_y = [(tile_of(z, lax.rem(y + d, ydim), core), lax.rem(y + d, ydim)) for d in far_first(ydim) if d]
    at_z = [(tile_of(lax.rem(z + d, zdim), y, core), lax.rem(z + d, zdim)) for d in far_first(zdim) if d]
    across = [k for k in far_first(groups) if k]

    rows = [(lax.rem(me + tiles - d, tiles), k) for k, d in enumerate((-2, -1, 1, 2))]
    level = jnp.minimum(grp * part, levels - part)

    peers = [{"tile": where} for where, _ in rows]
    peers += [{"tile": where} for where, _ in at_zc] + [{"tile": where} for where, _ in at_yc]
    peers += [{"grp": lax.rem(grp + k, groups)} for k in across]
    loads = [
        pltpu.make_async_copy(src, dst, load_sem.at[k])
        for k, (src, dst) in enumerate(
            (
                (fac, facv), (moi.at[pl.ds(level, part), 0, :], mine.at[0]), (kel.at[pl.ds(level, part), 0, :], mine.at[1]),
                (owner_h, owner), (arid_h, arid), (matt_h, matt), (share_h, share), (insol_h, insol), (mu_h, mu),
                (lit_h, lit), (spread_h, spread),
            )
        )
    ]
    for load in loads:
        load.start()

    barrier = pltpu.get_barrier_semaphore()
    for peer in peers:
        pl.semaphore_signal(barrier, inc=1, device_id=peer, device_id_type=MESH)

    loads[0].wait()
    tall = jnp.concatenate([facv[...], jnp.zeros((128 - gpts, facv.shape[1]), F32)], axis=0)
    fact[...] = tall.T
    step = CORES * CAP
    for k in range(zcdim):
        base = (k // CORES) * (ydim * step) + (k % CORES) * CAP
        out1a[k] = pair(fact, base, ydim, step)
    for k in range(ycdim):
        out1b[k] = pair(fact, k * CAP + 2, zdim, ydim * step)

    pl.semaphore_wait(barrier, len(peers))

    def spread_out(source, target, mine, partners, send, recv):
        copies = []
        for k, (where, other) in enumerate(partners):
            copies.append(
                remote(source.at[other], target.at[mine], send, recv, {"tile": where})
            )
            copies[-1].start()
        all_but_one = pl.ds(0, len(partners))
        return [remote(source.at[all_but_one], target.at[all_but_one], send, recv, {"tile": partners[0][0]})]

    phase1 = spread_out(out1a, mida, zc, at_zc, p1s.at[0], p1r.at[0])
    phase1 += spread_out(out1b, midb, yc, at_yc, p1s.at[1], p1r.at[1])
    halos = []
    for where, k in rows:
        for field, source in enumerate((moi, kel)):
            halos.append(
                remote(
                    source.at[pl.ds(level, part), 0, :], halo.at[k, field], hs.at[0], hr.at[0],
                    {"tile": where},
                )
            )
        if k in (1, 2):
            halos.append(remote(spread_h, coefs.at[k - 1], hs.at[1], hr.at[1], {"tile": where}))
    for copy in halos:
        copy.start()
    nearby = {"tile": rows[0][0]}
    halos = [
        remote(halo, halo, hs.at[0], hr.at[0], nearby),
        remote(coefs, coefs, hs.at[1], hr.at[1], nearby),
    ]

    mida[zc] = out1a[zc]
    midb[yc] = out1b[yc]

    for load in loads[3:]:
        load.wait()
    own = owner[...]
    place = lax.rem(own // CORES, ydim) * zcdim + (own // ycdim) * CORES + lax.rem(own, CORES)
    listed = lax.broadcasted_iota(jnp.int32, (tiles, cols), 0)
    hot = jnp.where(listed == own, 1.0, 0.0)
    before = jnp.where(
        lax.broadcasted_iota(jnp.int32, (cols, cols), 0) < lax.broadcasted_iota(jnp.int32, (cols, cols), 1),
        1.0,
        0.0,
    )
    earlier = jnp.dot(hot.astype(jnp.bfloat16), before.astype(jnp.bfloat16), preferred_element_type=F32)
    rank = jnp.sum(hot * earlier, axis=0, keepdims=True)
    hots[0:tiles] = jnp.where((listed == place) & (rank < 1.5), 1.0, 0.0).astype(jnp.bfloat16)
    hots[tiles : 2 * tiles] = jnp.where((listed == own) & (rank > 1.5), 1.0, 0.0).astype(jnp.bfloat16)
    odd = (rank == 1.0) | (rank == 3.0)

    for l in range(levels):
        dry[l] = jnp.broadcast_to(arid[:, l : l + 1] * (-LOG2E), (gpts, 128))

    def column(row):
        return jnp.broadcast_to(row[...], (128, gpts)).T

    share_c, insol_c, matt_c = column(share), column(insol), column(matt) * (-LOG2E)
    inv_mu = 1.0 / mu[...]
    sun = mu[...] * lit[...].astype(F32)

    def advance(x, coefficient, n, s):
        east, west = pltpu.roll(x, cols - 1, 1), pltpu.roll(x, 1, 1)
        return x + coefficient * (n + s + east + west - 4.0 * x)

    def arrive(copies):
        for copy in copies:
            copy.wait_recv()

    arrive(phase1)
    for k in range(ydim):
        out2a[k] = mida.reshape(tiles, 2 * SLOT)[pl.ds(k, zcdim, stride=ydim), :]
    for k in range(zdim):
        out2b[k] = midb.reshape(tiles, 2 * SLOT)[pl.ds(k, ycdim, stride=zdim), :]
    phase2 = spread_out(out2a, gota, y, at_y, p2s.at[0], p2r.at[0])
    phase2 += spread_out(out2b, gotb, z, at_z, p2s.at[1], p2r.at[1])
    gota[y] = out2a[y]
    gotb[z] = out2b[z]

    loads[1].wait()
    loads[2].wait()
    arrive(halos)
    shared = []
    for field, whole in enumerate((q2, t2)):
        x = [halo[0, field], halo[1, field], mine[field], halo[2, field], halo[3, field]]
        x = [jnp.where((me + d >= 0) & (me + d < tiles), v, 0.0) for d, v in zip(range(-2, 3), x)]
        north = jnp.where(me > 0, advance(x[1], coefs[0], x[0], x[2]), 0.0)
        south = jnp.where(me < tiles - 1, advance(x[3], coefs[1], x[2], x[4]), 0.0)
        own_row = advance(x[2], spread[...], x[1], x[3])
        here = whole.at[pl.ds(grp * part, part)]
        here[...] = advance(own_row, spread[...], north, south).reshape(part, 1, cols)
        for k in across:
            remote(here, here, xs.at[field], xr.at[field], {"grp": lax.rem(grp + k, groups)}).start()
        others = whole.at[pl.ds(0, (groups - 1) * part)]
        shared.append(
            remote(others, others, xs.at[field], xr.at[field], {"grp": lax.rem(grp + 1, groups)})
        )

    arrive(shared)
    last = (groups - 1) * part
    vapour = [
        pltpu.make_async_copy(q2.at[pl.ds(0, last)], vap_o.at[pl.ds(0, last)], vap_sem.at[0]),
        pltpu.make_async_copy(
            q2.at[pl.ds(last + gap, levels - last)], vap_o.at[pl.ds(last, levels - last)], vap_sem.at[1]
        ),
    ]
    for copy in vapour:
        copy.start()
    dts[0] = -t2[0]
    dts[1:last] = t2[0 : last - 1] - t2[1:last]
    dts[last] = t2[last - 1] - t2[last + gap]
    dts[last + 1 : levels] = t2[last + gap : levels + gap - 1] - t2[last + gap + 1 : levels + gap]
    dts[levels] = t2[levels + gap - 1]

    arrive(phase2)
    table = jnp.concatenate(
        [gota[...].reshape(tiles, 2 * SLOT), gotb[...].reshape(tiles, 2 * SLOT)], axis=0
    )
    picked = jnp.zeros((2 * SLOT, cols), F32)
    for _ in range(3):
        part = table.astype(jnp.bfloat16)
        table = table - part.astype(F32)
        picked = picked + lax.dot_general(
            part, hots[...], (((0,), (0,)), ((), ())), preferred_element_type=F32
        )
    chosen = jnp.where(odd, picked[SLOT : SLOT + gpts], picked[0:gpts])
    for half in range(cols // 128):
        wbuf[half] = chosen[:, 128 * half : 128 * half + 128] * matt_c

    ratio = insol_c / share_c
    folded = acc.reshape(8 * (levels + 1), 128)
    cut = levels // 16 * 8 + 8 * (levels > 32)
    pieces = [(cut, levels), (0, cut)] if 0 < cut < levels else [(0, levels)]
    reduce = []
    for half in range(cols // 128):
        lanes = pl.ds(128 * half, 128)
        w = wbuf[half]
        inv = inv_mu[:, 128 * half : 128 * half + 128]
        s0 = ratio * sun[:, 128 * half : 128 * half + 128]

        def down(l, carry, w=w, inv=inv, lanes=lanes):
            d, s = carry
            a = dry[l] + w * q2[jnp.where(l < last, l, l + gap), :, lanes]
            t, u = jnp.exp2(a), jnp.exp2(a * inv)
            m = t * d
            s = s * u
            tbuf[l] = t
            mbuf[l] = m + s
            return m + dts[l + 1, :, lanes], s

        def up(i, e, lanes=lanes):
            l = levels - 1 - i
            acc[l + 1] = fold8((mbuf[l] - e) * share_c)
            return tbuf[l] * e + dts_minus(l, lanes)

        def dts_minus(l, lanes):
            return -dts[l, :, lanes]

        start = jnp.broadcast_to(dts[0, :, lanes], (gpts, 128))
        lax.fori_loop(0, levels, down, (start, s0), unroll=30)
        e, done = jnp.zeros((gpts, 128), F32), 0
        for piece, (low, high) in enumerate(pieces):
            until = levels - max(low - 1, 0)
            e = lax.fori_loop(done, until, up, e, unroll=10)
            done = until
            if low == 0:
                acc[0] = fold8((s0 - e) * share_c)
            total = folded[pl.ds(8 * low, high + 1 - low, stride=8), :]
            for k in range(1, 8):
                total = total + folded[pl.ds(8 * low + k, high + 1 - low, stride=8), :]
            flux[low : high + 1, :] = total
            lines = pl.ds(low, high - low)
            gbuf[half, grp, lines] = flux[low:high, :] - flux[low + 1 : high + 1, :]
            here = gbuf.at[half, grp, lines]
            for k in across:
                remote(
                    here, here, gs.at[half, piece], gr.at[half, piece], {"grp": lax.rem(grp + k, groups)}
                ).start()
            others = gbuf.at[half, pl.ds(0, groups - 1), lines]
            reduce.append(
                remote(
                    others, others, gs.at[half, piece], gr.at[half, piece],
                    {"grp": lax.rem(grp + 1, groups)},
                )
            )

    for copy in vapour:
        copy.wait()
    for copy in halos + shared + phase1 + phase2:
        copy.wait_send()
    for half in range(cols // 128):
        lanes = pl.ds(128 * half, 128)
        for piece, (low, high) in enumerate(pieces):
            reduce[len(pieces) * half + piece].wait_recv()
            total = gbuf[half, 0, low:high]
            for k in range(1, groups):
                total = total + gbuf[half, k, low:high]
            total = (total * (1.0 / (groups * gpts))).reshape(high - low, 1, 128)
            heat_o[low:high, :, lanes] = total
            for first, stop, shift in ((low, min(high, last), 0), (max(low, last), high, gap)):
                if first < stop:
                    temp_o[first:stop, :, lanes] = (
                        t2[first + shift : stop + shift, :, lanes] + total[first - low : stop - low]
                    )
    for copy in reduce:
        copy.wait_send()


def finish_kernel(heat, temp, vap, heat_o, temp_o, vap_o, sem):
    copies = [
        pltpu.make_async_copy(value, out, sem.at[k])
        for k, (value, out) in enumerate(((heat, heat_o), (temp, temp_o), (vap, vap_o)))
    ]
    for copy in copies:
        copy.start()
    for copy in copies:
        copy.wait()


def on_device(
    tiles, ydim, groups,
    kelvin, moisture, spread, mu, lit, owner, fac, arid, matt, share, insol,
):
    levels, _, cols = kelvin.shape
    gpts, slots = fac.shape
    zcdim, ycdim = tiles // ydim, CORES * ydim
    zdim = zcdim // CORES
    vmem, hbm = pl.BlockSpec(memory_space=pltpu.VMEM), pl.BlockSpec(memory_space=pltpu.HBM)
    dma = pltpu.SemaphoreType.DMA
    part = -(-levels // (8 * groups)) * 8
    whole = pltpu.VMEM((groups * part, 1, cols), F32)
    out = pltpu.VMEM((levels, 1, cols), F32)
    heat, temp, vap = pl.pallas_call(
        functools.partial(radiation_kernel, (tiles, ydim, groups)),
        out_shape=(out, out, out),
        in_specs=[hbm] * 11,
        out_specs=(vmem, vmem, vmem),
        scratch_shapes=[
            pltpu.VMEM((gpts, slots), F32),
            pltpu.VMEM((1, cols), F32), pltpu.VMEM((1, cols), F32), pltpu.VMEM((1, cols), jnp.int32), pltpu.VMEM((1, cols), jnp.int32),
            pltpu.VMEM((gpts, levels), F32), pltpu.VMEM((1, gpts), F32), pltpu.VMEM((1, gpts), F32), pltpu.VMEM((1, gpts), F32),
            pltpu.VMEM((slots, 128), F32),
            pltpu.VMEM((zcdim, ydim, 128), F32), pltpu.VMEM((ycdim, zdim, 128), F32),
            pltpu.VMEM((zcdim, ydim, 128), F32), pltpu.VMEM((ycdim, zdim, 128), F32),
            pltpu.VMEM((ydim, zcdim, 128), F32), pltpu.VMEM((zdim, ycdim, 128), F32),
            pltpu.VMEM((ydim, zcdim, 128), F32), pltpu.VMEM((zdim, ycdim, 128), F32),
            pltpu.VMEM((2 * tiles, cols), jnp.bfloat16),
            pltpu.VMEM((2, part, cols), F32),
            pltpu.VMEM((4, 2, part, cols), F32),
            pltpu.VMEM((2, 1, cols), F32),
            whole, whole,
            pltpu.VMEM((levels + 1, 1, cols), F32),
            pltpu.VMEM((levels, gpts, 128), F32),
            pltpu.VMEM((levels, gpts, 128), F32),
            pltpu.VMEM((levels, gpts, 128), F32),
            pltpu.VMEM((levels + 1, 8, 128), F32),
            pltpu.VMEM((levels + 1, 128), F32),
            pltpu.VMEM((cols // 128, groups, levels, 128), F32),
            pltpu.VMEM((cols // 128, gpts, 128), F32),
            dma((11,)), dma((2,)), dma((2,)), dma((2,)), dma((2,)), dma((2,)),
            dma((2,)), dma((2,)), dma((2,)), dma((2,)),
            dma((cols // 128, 2)), dma((cols // 128, 2)),
        ],
        compiler_params=pltpu.CompilerParams(
            collective_id=0, has_side_effects=True, vmem_limit_bytes=56 * 2**20
        ),
    )(
        kelvin, moisture, spread, mu, lit, owner.reshape(1, cols), fac, arid,
        matt.reshape(1, gpts), share.reshape(1, gpts), insol.reshape(1, gpts),
    )
    out = jax.ShapeDtypeStruct(kelvin.shape, F32)
    return pl.pallas_call(
        finish_kernel,
        out_shape=(out, out, out),
        in_specs=[vmem] * 3,
        out_specs=(hbm,) * 3,
        scratch_shapes=[dma((3,))],
        compiler_params=pltpu.CompilerParams(vmem_limit_bytes=2**20),
    )(heat, temp, vap)


def solution(mesh):
    tiles, groups = mesh.shape["tile"], mesh.shape["grp"]
    ydim = min(ROWS_Y, tiles // (2 * CORES))
    wide, row = P(None, "tile", None), P("tile", None)
    in_specs = (
        wide, wide, row, row, row, row, P("grp", "tile"), P("grp", None), P("grp"), P("grp"), P("grp"),
    )
    return jax.shard_map(
        functools.partial(on_device, tiles, ydim, groups),
        mesh=mesh,
        in_specs=in_specs,
        out_specs=(wide, wide, wide),
        check_vma=False,
    )
```

```python
import functools
import math

import jax
import jax.numpy as jnp
from jax import lax
from jax.experimental import pallas as pl
from jax.experimental.pallas import tpu as pltpu
from jax.sharding import PartitionSpec as P

F32 = jnp.float32
CORES, ROWS_Y = 2, 8
CAP = 4
SLOT = 64
MESH = pl.DeviceIdType.MESH
LOG2E = math.log2(math.e)


def remote(src, dst, send, recv, where):
    return pltpu.make_async_remote_copy(
        src_ref=src, dst_ref=dst, send_sem=send, recv_sem=recv, device_id=where, device_id_type=MESH
    )


def far_first(n):
    return sorted(range(n), key=lambda d: -min(d, n - d))


def pair(rows, base, count, step):
    low, high = (rows[pl.ds(base + r, count, stride=step), :] for r in (0, 1))
    return low + pltpu.roll(high, SLOT, 1)


def fold8(x):
    parts = [x[8 * k : 8 * k + 8] for k in range(x.shape[0] // 8)]
    while len(parts) > 1:
        parts = [sum(parts[k : k + 2][1:], parts[k]) for k in range(0, len(parts), 2)]
    return parts[0]


def radiation_kernel(
    dims,
    kel, moi, spread_h, mu_h, lit_h, owner_h, fac, arid_h, matt_h, share_h, insol_h,
    heat_o, temp_o, vap_o,
    facv, spread, mu, lit, owner, arid, matt, share, insol, fact, out1a, out1b, mida, midb, out2a, out2b, gota, gotb, hots,
    mine, halo, coefs, q2, t2, dts,
    dry, tbuf, mbuf, acc, flux, gbuf, wbuf,
    load_sem, hs, hr, xs, xr, vap_sem, p1s, p1r, p2s, p2r, gs, gr,
):
    tiles, ydim, groups = dims
    zcdim, ycdim = tiles // ydim, CORES * ydim
    levels, _, cols = kel.shape
    part = halo.shape[2]
    gap = groups * part - levels
    gpts = arid.shape[0]
    me, grp = lax.axis_index("tile"), lax.axis_index("grp")
    core, y, z = lax.rem(me, CORES), lax.rem(me // CORES, ydim), me // (CORES * ydim)
    zdim = zcdim // CORES
    zc, yc = z * CORES + core, y * CORES + core

    def tile_of(a, b, c):
        return (a * ydim + b) * CORES + c

    near = [(d, c) for d in far_first(zdim) for c in (1, 0) if d or c]
    at_zc = []
    for d, c in near:
        zz, cc = lax.rem(z + d, zdim), lax.rem(core + c, CORES)
        at_zc.append((tile_of(zz, y, cc), zz * CORES + cc))
    at_yc = []
    for d, c in [(d, c) for d in far_first(ydim) for c in (1, 0) if d or c]:
        yy, cc = lax.rem(y + d, ydim), lax.rem(core + c, CORES)
        at_yc.append((tile_of(z, yy, cc), yy * CORES + cc))
    at_y = [(tile_of(z, lax.rem(y + d, ydim), core), lax.rem(y + d, ydim)) for d in far_first(ydim) if d]
    at_z = [(tile_of(lax.rem(z + d, zdim), y, core), lax.rem(z + d, zdim)) for d in far_first(zdim) if d]
    across = [k for k in far_first(groups) if k]

    rows = [(lax.rem(me + tiles - d, tiles), k) for k, d in enumerate((-2, -1, 1, 2))]
    level = jnp.minimum(grp * part, levels - part)

    peers = [{"tile": where} for where, _ in rows]
    peers += [{"tile": where} for where, _ in at_zc] + [{"tile": where} for where, _ in at_yc]
    peers += [{"grp": lax.rem(grp + k, groups)} for k in across]
    loads = [
        pltpu.make_async_copy(src, dst, load_sem.at[k])
        for k, (src, dst) in enumerate(
            (
                (fac, facv), (moi.at[pl.ds(level, part), 0, :], mine.at[0]), (kel.at[pl.ds(level, part), 0, :], mine.at[1]),
                (owner_h, owner), (arid_h, arid), (matt_h, matt), (share_h, share), (insol_h, insol), (mu_h, mu),
                (lit_h, lit), (spread_h, spread),
            )
        )
    ]
    for load in loads:
        load.start()

    barrier = pltpu.get_barrier_semaphore()
    for peer in peers:
        pl.semaphore_signal(barrier, inc=1, device_id=peer, device_id_type=MESH)

    loads[0].wait()
    tall = jnp.concatenate([facv[...], jnp.zeros((128 - gpts, facv.shape[1]), F32)], axis=0)
    fact[...] = tall.T
    step = CORES * CAP
    for k in range(zcdim):
        base = (k // CORES) * (ydim * step) + (k % CORES) * CAP
        out1a[k] = pair(fact, base, ydim, step)
    for k in range(ycdim):
        out1b[k] = pair(fact, k * CAP + 2, zdim, ydim * step)

    pl.semaphore_wait(barrier, len(peers))

    def spread_out(source, target, mine, partners, send, recv):
        copies = []
        for k, (where, other) in enumerate(partners):
            copies.append(
                remote(source.at[other], target.at[mine], send, recv, {"tile": where})
            )
            copies[-1].start()
        all_but_one = pl.ds(0, len(partners))
        return [remote(source.at[all_but_one], target.at[all_but_one], send, recv, {"tile": partners[0][0]})]

    phase1 = spread_out(out1a, mida, zc, at_zc, p1s.at[0], p1r.at[0])
    phase1 += spread_out(out1b, midb, yc, at_yc, p1s.at[1], p1r.at[1])
    halos = []
    for where, k in rows:
        for field, source in enumerate((moi, kel)):
            halos.append(
                remote(
                    source.at[pl.ds(level, part), 0, :], halo.at[k, field], hs.at[0], hr.at[0],
                    {"tile": where},
                )
            )
        if k in (1, 2):
            halos.append(remote(spread_h, coefs.at[k - 1], hs.at[1], hr.at[1], {"tile": where}))
    for copy in halos:
        copy.start()
    nearby = {"tile": rows[0][0]}
    halos = [
        remote(halo, halo, hs.at[0], hr.at[0], nearby),
        remote(coefs, coefs, hs.at[1], hr.at[1], nearby),
    ]

    mida[zc] = out1a[zc]
    midb[yc] = out1b[yc]

    for load in loads[3:]:
        load.wait()
    own = owner[...]
    place = lax.rem(own // CORES, ydim) * zcdim + (own // ycdim) * CORES + lax.rem(own, CORES)
    listed = lax.broadcasted_iota(jnp.int32, (tiles, cols), 0)
    hot = jnp.where(listed == own, 1.0, 0.0)
    before = jnp.where(
        lax.broadcasted_iota(jnp.int32, (cols, cols), 0) < lax.broadcasted_iota(jnp.int32, (cols, cols), 1),
        1.0,
        0.0,
    )
    earlier = jnp.dot(hot.astype(jnp.bfloat16), before.astype(jnp.bfloat16), preferred_element_type=F32)
    rank = jnp.sum(hot * earlier, axis=0, keepdims=True)
    hots[0:tiles] = jnp.where((listed == place) & (rank < 1.5), 1.0, 0.0).astype(jnp.bfloat16)
    hots[tiles : 2 * tiles] = jnp.where((listed == own) & (rank > 1.5), 1.0, 0.0).astype(jnp.bfloat16)
    odd = (rank == 1.0) | (rank == 3.0)

    for l in range(levels):
        dry[l] = jnp.broadcast_to(arid[:, l : l + 1] * (-LOG2E), (gpts, 128))

    def column(row):
        return jnp.broadcast_to(row[...], (128, gpts)).T

    share_c, insol_c, matt_c = column(share), column(insol), column(matt) * (-LOG2E)
    inv_mu = 1.0 / mu[...]
    sun = mu[...] * lit[...].astype(F32)

    def advance(x, coefficient, n, s):
        east, west = pltpu.roll(x, cols - 1, 1), pltpu.roll(x, 1, 1)
        return x + coefficient * (n + s + east + west - 4.0 * x)

    def arrive(copies):
        for copy in copies:
            copy.wait_recv()

    arrive(phase1)
    for k in range(ydim):
        out2a[k] = mida.reshape(tiles, 2 * SLOT)[pl.ds(k, zcdim, stride=ydim), :]
    for k in range(zdim):
        out2b[k] = midb.reshape(tiles, 2 * SLOT)[pl.ds(k, ycdim, stride=zdim), :]
    phase2 = spread_out(out2a, gota, y, at_y, p2s.at[0], p2r.at[0])
    phase2 += spread_out(out2b, gotb, z, at_z, p2s.at[1], p2r.at[1])
    gota[y] = out2a[y]
    gotb[z] = out2b[z]

    loads[1].wait()
    loads[2].wait()
    arrive(halos)
    shared = []
    for field, whole in enumerate((q2, t2)):
        x = [halo[0, field], halo[1, field], mine[field], halo[2, field], halo[3, field]]
        x = [jnp.where((me + d >= 0) & (me + d < tiles), v, 0.0) for d, v in zip(range(-2, 3), x)]
        north = jnp.where(me > 0, advance(x[1], coefs[0], x[0], x[2]), 0.0)
        south = jnp.where(me < tiles - 1, advance(x[3], coefs[1], x[2], x[4]), 0.0)
        own_row = advance(x[2], spread[...], x[1], x[3])
        here = whole.at[pl.ds(grp * part, part)]
        here[...] = advance(own_row, spread[...], north, south).reshape(part, 1, cols)
        for k in across:
            remote(here, here, xs.at[field], xr.at[field], {"grp": lax.rem(grp + k, groups)}).start()
        others = whole.at[pl.ds(0, (groups - 1) * part)]
        shared.append(
            remote(others, others, xs.at[field], xr.at[field], {"grp": lax.rem(grp + 1, groups)})
        )

    arrive(shared)
    last = (groups - 1) * part
    vapour = [
        pltpu.make_async_copy(q2.at[pl.ds(0, last)], vap_o.at[pl.ds(0, last)], vap_sem.at[0]),
        pltpu.make_async_copy(
            q2.at[pl.ds(last + gap, levels - last)], vap_o.at[pl.ds(last, levels - last)], vap_sem.at[1]
        ),
    ]
    for copy in vapour:
        copy.start()
    dts[0] = -t2[0]
    dts[1:last] = t2[0 : last - 1] - t2[1:last]
    dts[last] = t2[last - 1] - t2[last + gap]
    dts[last + 1 : levels] = t2[last + gap : levels + gap - 1] - t2[last + gap + 1 : levels + gap]
    dts[levels] = t2[levels + gap - 1]

    arrive(phase2)
    table = jnp.concatenate(
        [gota[...].reshape(tiles, 2 * SLOT), gotb[...].reshape(tiles, 2 * SLOT)], axis=0
    )
    picked = jnp.zeros((2 * SLOT, cols), F32)
    for _ in range(3):
        part = table.astype(jnp.bfloat16)
        table = table - part.astype(F32)
        picked = picked + lax.dot_general(
            part, hots[...], (((0,), (0,)), ((), ())), preferred_element_type=F32
        )
    chosen = jnp.where(odd, picked[SLOT : SLOT + gpts], picked[0:gpts])
    for half in range(cols // 128):
        wbuf[half] = chosen[:, 128 * half : 128 * half + 128] * matt_c

    ratio = insol_c / share_c
    folded = acc.reshape(8 * (levels + 1), 128)
    cut = levels // 16 * 8 + 8 * (levels > 32)
    pieces = [[(0, levels)]] * (cols // 128 - 1) + [[(cut, levels), (0, cut)]]
    reduce = []
    for half in range(cols // 128):
        lanes = pl.ds(128 * half, 128)
        w = wbuf[half]
        inv = inv_mu[:, 128 * half : 128 * half + 128]
        s0 = ratio * sun[:, 128 * half : 128 * half + 128]

        def down(l, carry, w=w, inv=inv, lanes=lanes):
            d, s = carry
            a = dry[l] + w * q2[jnp.where(l < last, l, l + gap), :, lanes]
            t, u = jnp.exp2(a), jnp.exp2(a * inv)
            m = t * d
            s = s * u
            tbuf[l] = t
            mbuf[l] = m + s
            return m + dts[l + 1, :, lanes], s

        def up(i, e, lanes=lanes):
            l = levels - 1 - i
            acc[l + 1] = fold8((mbuf[l] - e) * share_c)
            return tbuf[l] * e + dts_minus(l, lanes)

        def dts_minus(l, lanes):
            return -dts[l, :, lanes]

        start = jnp.broadcast_to(dts[0, :, lanes], (gpts, 128))
        lax.fori_loop(0, levels, down, (start, s0), unroll=30)
        e, done = jnp.zeros((gpts, 128), F32), 0
        for piece, (low, high) in enumerate(pieces[half]):
            until = levels if low == 0 else min(-(-(levels + 1 - low) // 10) * 10, levels)
            e = lax.fori_loop(done, until, up, e, unroll=10)
            done = until
            if low == 0:
                acc[0] = fold8((s0 - e) * share_c)
            total = folded[pl.ds(8 * low, high + 1 - low, stride=8), :]
            for k in range(1, 8):
                total = total + folded[pl.ds(8 * low + k, high + 1 - low, stride=8), :]
            flux[low : high + 1, :] = total
            lines = pl.ds(low, high - low)
            gbuf[half, grp, lines] = flux[low:high, :] - flux[low + 1 : high + 1, :]
            here = gbuf.at[half, grp, lines]
            for k in across:
                remote(
                    here, here, gs.at[half, piece], gr.at[half, piece], {"grp": lax.rem(grp + k, groups)}
                ).start()
            others = gbuf.at[half, pl.ds(0, groups - 1), lines]
            reduce.append(
                remote(
                    others, others, gs.at[half, piece], gr.at[half, piece],
                    {"grp": lax.rem(grp + 1, groups)},
                )
            )

    for copy in vapour:
        copy.wait()
    for copy in halos + shared + phase1 + phase2:
        copy.wait_send()
    for half in range(cols // 128):
        lanes = pl.ds(128 * half, 128)
        for piece, (low, high) in enumerate(pieces[half]):
            reduce[half + piece].wait_recv()
            total = gbuf[half, 0, low:high]
            for k in range(1, groups):
                total = total + gbuf[half, k, low:high]
            total = (total * (1.0 / (groups * gpts))).reshape(high - low, 1, 128)
            heat_o[low:high, :, lanes] = total
            for first, stop, shift in ((low, min(high, last), 0), (max(low, last), high, gap)):
                if first < stop:
                    temp_o[first:stop, :, lanes] = (
                        t2[first + shift : stop + shift, :, lanes] + total[first - low : stop - low]
                    )
    for copy in reduce:
        copy.wait_send()


def finish_kernel(heat, temp, vap, heat_o, temp_o, vap_o, sem):
    copies = [
        pltpu.make_async_copy(value, out, sem.at[k])
        for k, (value, out) in enumerate(((heat, heat_o), (temp, temp_o), (vap, vap_o)))
    ]
    for copy in copies:
        copy.start()
    for copy in copies:
        copy.wait()


def on_device(
    tiles, ydim, groups,
    kelvin, moisture, spread, mu, lit, owner, fac, arid, matt, share, insol,
):
    levels, _, cols = kelvin.shape
    gpts, slots = fac.shape
    zcdim, ycdim = tiles // ydim, CORES * ydim
    zdim = zcdim // CORES
    vmem, hbm = pl.BlockSpec(memory_space=pltpu.VMEM), pl.BlockSpec(memory_space=pltpu.HBM)
    dma = pltpu.SemaphoreType.DMA
    part = -(-levels // (8 * groups)) * 8
    whole = pltpu.VMEM((groups * part, 1, cols), F32)
    out = pltpu.VMEM((levels, 1, cols), F32)
    heat, temp, vap = pl.pallas_call(
        functools.partial(radiation_kernel, (tiles, ydim, groups)),
        out_shape=(out, out, out),
        in_specs=[hbm] * 11,
        out_specs=(vmem, vmem, vmem),
        scratch_shapes=[
            pltpu.VMEM((gpts, slots), F32),
            pltpu.VMEM((1, cols), F32), pltpu.VMEM((1, cols), F32), pltpu.VMEM((1, cols), jnp.int32), pltpu.VMEM((1, cols), jnp.int32),
            pltpu.VMEM((gpts, levels), F32), pltpu.VMEM((1, gpts), F32), pltpu.VMEM((1, gpts), F32), pltpu.VMEM((1, gpts), F32),
            pltpu.VMEM((slots, 128), F32),
            pltpu.VMEM((zcdim, ydim, 128), F32), pltpu.VMEM((ycdim, zdim, 128), F32),
            pltpu.VMEM((zcdim, ydim, 128), F32), pltpu.VMEM((ycdim, zdim, 128), F32),
            pltpu.VMEM((ydim, zcdim, 128), F32), pltpu.VMEM((zdim, ycdim, 128), F32),
            pltpu.VMEM((ydim, zcdim, 128), F32), pltpu.VMEM((zdim, ycdim, 128), F32),
            pltpu.VMEM((2 * tiles, cols), jnp.bfloat16),
            pltpu.VMEM((2, part, cols), F32),
            pltpu.VMEM((4, 2, part, cols), F32),
            pltpu.VMEM((2, 1, cols), F32),
            whole, whole,
            pltpu.VMEM((levels + 1, 1, cols), F32),
            pltpu.VMEM((levels, gpts, 128), F32),
            pltpu.VMEM((levels, gpts, 128), F32),
            pltpu.VMEM((levels, gpts, 128), F32),
            pltpu.VMEM((levels + 1, 8, 128), F32),
            pltpu.VMEM((levels + 1, 128), F32),
            pltpu.VMEM((cols // 128, groups, levels, 128), F32),
            pltpu.VMEM((cols // 128, gpts, 128), F32),
            dma((11,)), dma((2,)), dma((2,)), dma((2,)), dma((2,)), dma((2,)),
            dma((2,)), dma((2,)), dma((2,)), dma((2,)),
            dma((cols // 128, 2)), dma((cols // 128, 2)),
        ],
        compiler_params=pltpu.CompilerParams(
            collective_id=0, has_side_effects=True, vmem_limit_bytes=56 * 2**20
        ),
    )(
        kelvin, moisture, spread, mu, lit, owner.reshape(1, cols), fac, arid,
        matt.reshape(1, gpts), share.reshape(1, gpts), insol.reshape(1, gpts),
    )
    out = jax.ShapeDtypeStruct(kelvin.shape, F32)
    return pl.pallas_call(
        finish_kernel,
        out_shape=(out, out, out),
        in_specs=[vmem] * 3,
        out_specs=(hbm,) * 3,
        scratch_shapes=[dma((3,))],
        compiler_params=pltpu.CompilerParams(vmem_limit_bytes=2**20),
    )(heat, temp, vap)


def solution(mesh):
    tiles, groups = mesh.shape["tile"], mesh.shape["grp"]
    ydim = min(ROWS_Y, tiles // (2 * CORES))
    wide, row = P(None, "tile", None), P("tile", None)
    in_specs = (
        wide, wide, row, row, row, row, P("grp", "tile"), P("grp", None), P("grp"), P("grp"), P("grp"),
    )
    return jax.shard_map(
        functools.partial(on_device, tiles, ydim, groups),
        mesh=mesh,
        in_specs=in_specs,
        out_specs=(wide, wide, wide),
        check_vma=False,
    )
```

```python
import functools
import math

import jax
import jax.numpy as jnp
from jax import lax
from jax.experimental import pallas as pl
from jax.experimental.pallas import tpu as pltpu
from jax.sharding import PartitionSpec as P

F32 = jnp.float32
CORES, ROWS_Y = 2, 8
CAP = 4
SLOT = 64
MESH = pl.DeviceIdType.MESH
LOG2E = math.log2(math.e)


def remote(src, dst, send, recv, where):
    return pltpu.make_async_remote_copy(
        src_ref=src, dst_ref=dst, send_sem=send, recv_sem=recv, device_id=where, device_id_type=MESH
    )


def far_first(n):
    return sorted(range(n), key=lambda d: -min(d, n - d))


def pair(rows, base, count, step):
    low, high = (rows[pl.ds(base + r, count, stride=step), :] for r in (0, 1))
    return low + pltpu.roll(high, SLOT, 1)


def fold8(x):
    parts = [x[8 * k : 8 * k + 8] for k in range(x.shape[0] // 8)]
    while len(parts) > 1:
        parts = [sum(parts[k : k + 2][1:], parts[k]) for k in range(0, len(parts), 2)]
    return parts[0]


def radiation_kernel(
    dims,
    kel, moi, spread_h, mu_h, lit_h, owner_h, fac, arid_h, matt_h, share_h, insol_h,
    heat_o, temp_o, vap_o,
    facv, spread, mu, lit, owner, arid, matt, share, insol, fact, out1a, out1b, mida, midb, out2a, out2b, gota, gotb, hots,
    mine, halo, coefs, q2, t2, dts,
    dry, tbuf, mbuf, acc, flux, gbuf, wbuf,
    load_sem, hs, hr, xs, xr, vap_sem, p1s, p1r, p2s, p2r, gs, gr,
):
    tiles, ydim, groups = dims
    zcdim, ycdim = tiles // ydim, CORES * ydim
    levels, _, cols = kel.shape
    part = halo.shape[2]
    gap = groups * part - levels
    gpts = arid.shape[0]
    me, grp = lax.axis_index("tile"), lax.axis_index("grp")
    core, y, z = lax.rem(me, CORES), lax.rem(me // CORES, ydim), me // (CORES * ydim)
    zdim = zcdim // CORES
    zc, yc = z * CORES + core, y * CORES + core

    def tile_of(a, b, c):
        return (a * ydim + b) * CORES + c

    near = [(d, c) for d in far_first(zdim) for c in (1, 0) if d or c]
    at_zc = []
    for d, c in near:
        zz, cc = lax.rem(z + d, zdim), lax.rem(core + c, CORES)
        at_zc.append((tile_of(zz, y, cc), zz * CORES + cc))
    at_yc = []
    for d, c in [(d, c) for d in far_first(ydim) for c in (1, 0) if d or c]:
        yy, cc = lax.rem(y + d, ydim), lax.rem(core + c, CORES)
        at_yc.append((tile_of(z, yy, cc), yy * CORES + cc))
    at_y = [(tile_of(z, lax.rem(y + d, ydim), core), lax.rem(y + d, ydim)) for d in far_first(ydim) if d]
    at_z = [(tile_of(lax.rem(z + d, zdim), y, core), lax.rem(z + d, zdim)) for d in far_first(zdim) if d]
    across = [k for k in far_first(groups) if k]

    rows = [(lax.rem(me + tiles - d, tiles), k) for k, d in enumerate((-2, -1, 1, 2))]
    level = jnp.minimum(grp * part, levels - part)

    peers = [{"tile": where} for where, _ in rows]
    peers += [{"tile": where} for where, _ in at_zc] + [{"tile": where} for where, _ in at_yc]
    peers += [{"grp": lax.rem(grp + k, groups)} for k in across]
    loads = [
        pltpu.make_async_copy(src, dst, load_sem.at[k])
        for k, (src, dst) in enumerate(
            (
                (fac, facv), (moi.at[pl.ds(level, part), 0, :], mine.at[0]), (kel.at[pl.ds(level, part), 0, :], mine.at[1]),
                (owner_h, owner), (arid_h, arid), (matt_h, matt), (share_h, share), (insol_h, insol), (mu_h, mu),
                (lit_h, lit), (spread_h, spread),
            )
        )
    ]
    for load in loads:
        load.start()

    barrier = pltpu.get_barrier_semaphore()
    for peer in peers:
        pl.semaphore_signal(barrier, inc=1, device_id=peer, device_id_type=MESH)

    loads[0].wait()
    tall = jnp.concatenate([facv[...], jnp.zeros((128 - gpts, facv.shape[1]), F32)], axis=0)
    fact[...] = tall.T
    step = CORES * CAP
    for k in range(zcdim):
        base = (k // CORES) * (ydim * step) + (k % CORES) * CAP
        out1a[k] = pair(fact, base, ydim, step)
    for k in range(ycdim):
        out1b[k] = pair(fact, k * CAP + 2, zdim, ydim * step)

    pl.semaphore_wait(barrier, len(peers))

    def spread_out(source, target, mine, partners, send, recv):
        copies = []
        for k, (where, other) in enumerate(partners):
            copies.append(
                remote(source.at[other], target.at[mine], send, recv, {"tile": where})
            )
            copies[-1].start()
        all_but_one = pl.ds(0, len(partners))
        return [remote(source.at[all_but_one], target.at[all_but_one], send, recv, {"tile": partners[0][0]})]

    phase1 = spread_out(out1a, mida, zc, at_zc, p1s.at[0], p1r.at[0])
    phase1 += spread_out(out1b, midb, yc, at_yc, p1s.at[1], p1r.at[1])
    halos = []
    for where, k in rows:
        for field, source in enumerate((moi, kel)):
            halos.append(
                remote(
                    source.at[pl.ds(level, part), 0, :], halo.at[k, field], hs.at[0], hr.at[0],
                    {"tile": where},
                )
            )
        if k in (1, 2):
            halos.append(remote(spread_h, coefs.at[k - 1], hs.at[1], hr.at[1], {"tile": where}))
    for copy in halos:
        copy.start()
    nearby = {"tile": rows[0][0]}
    halos = [
        remote(halo, halo, hs.at[0], hr.at[0], nearby),
        remote(coefs, coefs, hs.at[1], hr.at[1], nearby),
    ]

    mida[zc] = out1a[zc]
    midb[yc] = out1b[yc]

    for load in loads[3:]:
        load.wait()
    own = owner[...]
    place = lax.rem(own // CORES, ydim) * zcdim + (own // ycdim) * CORES + lax.rem(own, CORES)
    listed = lax.broadcasted_iota(jnp.int32, (tiles, cols), 0)
    hot = jnp.where(listed == own, 1.0, 0.0)
    before = jnp.where(
        lax.broadcasted_iota(jnp.int32, (cols, cols), 0) < lax.broadcasted_iota(jnp.int32, (cols, cols), 1),
        1.0,
        0.0,
    )
    earlier = jnp.dot(hot.astype(jnp.bfloat16), before.astype(jnp.bfloat16), preferred_element_type=F32)
    rank = jnp.sum(hot * earlier, axis=0, keepdims=True)
    hots[0:tiles] = jnp.where((listed == place) & (rank < 1.5), 1.0, 0.0).astype(jnp.bfloat16)
    hots[tiles : 2 * tiles] = jnp.where((listed == own) & (rank > 1.5), 1.0, 0.0).astype(jnp.bfloat16)
    odd = (rank == 1.0) | (rank == 3.0)

    for l in range(levels):
        dry[l] = jnp.broadcast_to(arid[:, l : l + 1] * (-LOG2E), (gpts, 128))

    def column(row):
        return jnp.broadcast_to(row[...], (128, gpts)).T

    share_c, insol_c, matt_c = column(share), column(insol), column(matt) * (-LOG2E)
    inv_mu = 1.0 / mu[...]
    sun = mu[...] * lit[...].astype(F32)

    def advance(x, coefficient, n, s):
        east, west = pltpu.roll(x, cols - 1, 1), pltpu.roll(x, 1, 1)
        return x + coefficient * (n + s + east + west - 4.0 * x)

    def arrive(copies):
        for copy in copies:
            copy.wait_recv()

    arrive(phase1[:1])
    for k in range(ydim):
        out2a[k] = mida.reshape(tiles, 2 * SLOT)[pl.ds(k, zcdim, stride=ydim), :]
    phase2 = spread_out(out2a, gota, y, at_y, p2s.at[0], p2r.at[0])
    arrive(phase1[1:])
    for k in range(zdim):
        out2b[k] = midb.reshape(tiles, 2 * SLOT)[pl.ds(k, ycdim, stride=zdim), :]
    phase2 += spread_out(out2b, gotb, z, at_z, p2s.at[1], p2r.at[1])
    gota[y] = out2a[y]
    gotb[z] = out2b[z]

    loads[1].wait()
    loads[2].wait()
    arrive(halos)
    shared = []
    for field, whole in enumerate((q2, t2)):
        x = [halo[0, field], halo[1, field], mine[field], halo[2, field], halo[3, field]]
        x = [jnp.where((me + d >= 0) & (me + d < tiles), v, 0.0) for d, v in zip(range(-2, 3), x)]
        north = jnp.where(me > 0, advance(x[1], coefs[0], x[0], x[2]), 0.0)
        south = jnp.where(me < tiles - 1, advance(x[3], coefs[1], x[2], x[4]), 0.0)
        own_row = advance(x[2], spread[...], x[1], x[3])
        here = whole.at[pl.ds(grp * part, part)]
        here[...] = advance(own_row, spread[...], north, south).reshape(part, 1, cols)
        for k in across:
            remote(here, here, xs.at[field], xr.at[field], {"grp": lax.rem(grp + k, groups)}).start()
        others = whole.at[pl.ds(0, (groups - 1) * part)]
        shared.append(
            remote(others, others, xs.at[field], xr.at[field], {"grp": lax.rem(grp + 1, groups)})
        )

    arrive(shared)
    last = (groups - 1) * part
    vapour = [
        pltpu.make_async_copy(q2.at[pl.ds(0, last)], vap_o.at[pl.ds(0, last)], vap_sem.at[0]),
        pltpu.make_async_copy(
            q2.at[pl.ds(last + gap, levels - last)], vap_o.at[pl.ds(last, levels - last)], vap_sem.at[1]
        ),
    ]
    for copy in vapour:
        copy.start()
    dts[0] = -t2[0]
    dts[1:last] = t2[0 : last - 1] - t2[1:last]
    dts[last] = t2[last - 1] - t2[last + gap]
    dts[last + 1 : levels] = t2[last + gap : levels + gap - 1] - t2[last + gap + 1 : levels + gap]
    dts[levels] = t2[levels + gap - 1]

    arrive(phase2)
    table = jnp.concatenate(
        [gota[...].reshape(tiles, 2 * SLOT), gotb[...].reshape(tiles, 2 * SLOT)], axis=0
    )
    picked = jnp.zeros((2 * SLOT, cols), F32)
    for _ in range(3):
        part = table.astype(jnp.bfloat16)
        table = table - part.astype(F32)
        picked = picked + lax.dot_general(
            part, hots[...], (((0,), (0,)), ((), ())), preferred_element_type=F32
        )
    chosen = jnp.where(odd, picked[SLOT : SLOT + gpts], picked[0:gpts])
    for half in range(cols // 128):
        wbuf[half] = chosen[:, 128 * half : 128 * half + 128] * matt_c

    ratio = insol_c / share_c
    folded = acc.reshape(8 * (levels + 1), 128)
    cut = levels // 16 * 8 + 8 * (levels > 32)
    pieces = [(cut, levels), (0, cut)] if 0 < cut < levels else [(0, levels)]
    reduce = []
    for half in range(cols // 128):
        lanes = pl.ds(128 * half, 128)
        w = wbuf[half]
        inv = inv_mu[:, 128 * half : 128 * half + 128]
        s0 = ratio * sun[:, 128 * half : 128 * half + 128]

        def down(l, carry, w=w, inv=inv, lanes=lanes):
            d, s = carry
            a = dry[l] + w * q2[jnp.where(l < last, l, l + gap), :, lanes]
            t, u = jnp.exp2(a), jnp.exp2(a * inv)
            m = t * d
            s = s * u
            tbuf[l] = t
            mbuf[l] = m + s
            return m + dts[l + 1, :, lanes], s

        def up(i, e, lanes=lanes):
            l = levels - 1 - i
            acc[l + 1] = fold8((mbuf[l] - e) * share_c)
            return tbuf[l] * e + dts_minus(l, lanes)

        def dts_minus(l, lanes):
            return -dts[l, :, lanes]

        start = jnp.broadcast_to(dts[0, :, lanes], (gpts, 128))
        lax.fori_loop(0, levels, down, (start, s0), unroll=45)
        e, done = jnp.zeros((gpts, 128), F32), 0
        for piece, (low, high) in enumerate(pieces):
            until = levels - max(low - 1, 0)
            e = lax.fori_loop(done, until, up, e, unroll=10)
            done = until
            if low == 0:
                acc[0] = fold8((s0 - e) * share_c)
            total = folded[pl.ds(8 * low, high + 1 - low, stride=8), :]
            for k in range(1, 8):
                total = total + folded[pl.ds(8 * low + k, high + 1 - low, stride=8), :]
            flux[low : high + 1, :] = total
            lines = pl.ds(low, high - low)
            gbuf[half, grp, lines] = flux[low:high, :] - flux[low + 1 : high + 1, :]
            here = gbuf.at[half, grp, lines]
            for k in across:
                remote(
                    here, here, gs.at[half, piece], gr.at[half, piece], {"grp": lax.rem(grp + k, groups)}
                ).start()
            others = gbuf.at[half, pl.ds(0, groups - 1), lines]
            reduce.append(
                remote(
                    others, others, gs.at[half, piece], gr.at[half, piece],
                    {"grp": lax.rem(grp + 1, groups)},
                )
            )

    for copy in vapour:
        copy.wait()
    for copy in halos + shared + phase1 + phase2:
        copy.wait_send()
    for half in range(cols // 128):
        lanes = pl.ds(128 * half, 128)
        for piece, (low, high) in enumerate(pieces):
            reduce[len(pieces) * half + piece].wait_recv()
            total = gbuf[half, 0, low:high]
            for k in range(1, groups):
                total = total + gbuf[half, k, low:high]
            total = (total * (1.0 / (groups * gpts))).reshape(high - low, 1, 128)
            heat_o[low:high, :, lanes] = total
            for first, stop, shift in ((low, min(high, last), 0), (max(low, last), high, gap)):
                if first < stop:
                    temp_o[first:stop, :, lanes] = (
                        t2[first + shift : stop + shift, :, lanes] + total[first - low : stop - low]
                    )
    for copy in reduce:
        copy.wait_send()


def finish_kernel(heat, temp, vap, heat_o, temp_o, vap_o, sem):
    copies = [
        pltpu.make_async_copy(value, out, sem.at[k])
        for k, (value, out) in enumerate(((heat, heat_o), (temp, temp_o), (vap, vap_o)))
    ]
    for copy in copies:
        copy.start()
    for copy in copies:
        copy.wait()


def on_device(
    tiles, ydim, groups,
    kelvin, moisture, spread, mu, lit, owner, fac, arid, matt, share, insol,
):
    levels, _, cols = kelvin.shape
    gpts, slots = fac.shape
    zcdim, ycdim = tiles // ydim, CORES * ydim
    zdim = zcdim // CORES
    vmem, hbm = pl.BlockSpec(memory_space=pltpu.VMEM), pl.BlockSpec(memory_space=pltpu.HBM)
    dma = pltpu.SemaphoreType.DMA
    part = -(-levels // (8 * groups)) * 8
    whole = pltpu.VMEM((groups * part, 1, cols), F32)
    out = pltpu.VMEM((levels, 1, cols), F32)
    heat, temp, vap = pl.pallas_call(
        functools.partial(radiation_kernel, (tiles, ydim, groups)),
        out_shape=(out, out, out),
        in_specs=[hbm] * 11,
        out_specs=(vmem, vmem, vmem),
        scratch_shapes=[
            pltpu.VMEM((gpts, slots), F32),
            pltpu.VMEM((1, cols), F32), pltpu.VMEM((1, cols), F32), pltpu.VMEM((1, cols), jnp.int32), pltpu.VMEM((1, cols), jnp.int32),
            pltpu.VMEM((gpts, levels), F32), pltpu.VMEM((1, gpts), F32), pltpu.VMEM((1, gpts), F32), pltpu.VMEM((1, gpts), F32),
            pltpu.VMEM((slots, 128), F32),
            pltpu.VMEM((zcdim, ydim, 128), F32), pltpu.VMEM((ycdim, zdim, 128), F32),
            pltpu.VMEM((zcdim, ydim, 128), F32), pltpu.VMEM((ycdim, zdim, 128), F32),
            pltpu.VMEM((ydim, zcdim, 128), F32), pltpu.VMEM((zdim, ycdim, 128), F32),
            pltpu.VMEM((ydim, zcdim, 128), F32), pltpu.VMEM((zdim, ycdim, 128), F32),
            pltpu.VMEM((2 * tiles, cols), jnp.bfloat16),
            pltpu.VMEM((2, part, cols), F32),
            pltpu.VMEM((4, 2, part, cols), F32),
            pltpu.VMEM((2, 1, cols), F32),
            whole, whole,
            pltpu.VMEM((levels + 1, 1, cols), F32),
            pltpu.VMEM((levels, gpts, 128), F32),
            pltpu.VMEM((levels, gpts, 128), F32),
            pltpu.VMEM((levels, gpts, 128), F32),
            pltpu.VMEM((levels + 1, 8, 128), F32),
            pltpu.VMEM((levels + 1, 128), F32),
            pltpu.VMEM((cols // 128, groups, levels, 128), F32),
            pltpu.VMEM((cols // 128, gpts, 128), F32),
            dma((11,)), dma((2,)), dma((2,)), dma((2,)), dma((2,)), dma((2,)),
            dma((2,)), dma((2,)), dma((2,)), dma((2,)),
            dma((cols // 128, 2)), dma((cols // 128, 2)),
        ],
        compiler_params=pltpu.CompilerParams(
            collective_id=0, has_side_effects=True, vmem_limit_bytes=56 * 2**20
        ),
    )(
        kelvin, moisture, spread, mu, lit, owner.reshape(1, cols), fac, arid,
        matt.reshape(1, gpts), share.reshape(1, gpts), insol.reshape(1, gpts),
    )
    out = jax.ShapeDtypeStruct(kelvin.shape, F32)
    return pl.pallas_call(
        finish_kernel,
        out_shape=(out, out, out),
        in_specs=[vmem] * 3,
        out_specs=(hbm,) * 3,
        scratch_shapes=[dma((3,))],
        compiler_params=pltpu.CompilerParams(vmem_limit_bytes=2**20),
    )(heat, temp, vap)


def solution(mesh):
    tiles, groups = mesh.shape["tile"], mesh.shape["grp"]
    ydim = min(ROWS_Y, tiles // (2 * CORES))
    wide, row = P(None, "tile", None), P("tile", None)
    in_specs = (
        wide, wide, row, row, row, row, P("grp", "tile"), P("grp", None), P("grp"), P("grp"), P("grp"),
    )
    return jax.shard_map(
        functools.partial(on_device, tiles, ydim, groups),
        mesh=mesh,
        in_specs=in_specs,
        out_specs=(wide, wide, wide),
        check_vma=False,
    )
```
